512 devices in a mesh: member: 16 (over z_hi, x), space: 32 (over z_lo, y, core).
Axes of the slice: x: 4, y: 8, z: 8 (z_hi: 4, z_lo: 2; z = z_hi * 2 + z_lo), core: 2. Of those that a mesh axis runs over, the one named last changes fastest.
Arguments:
- tokens: bfloat16 [16, 32, 256, 1536], P('member', None, 'space'), may hold values from -6 to 6
- norm_gain: float32 [1536], replicated, may hold values from 0.1 to 1.9
- w_qkv: bfloat16 [1536, 2304], P('space'), may hold values from -0.15625 to 0.15625
- w_out: bfloat16 [768, 1536], P('space'), may hold values from -0.21875 to 0.21875
- rel_bias: float32 [24, 64, 64], replicated, may hold values from -4 to 402
- w_decode: bfloat16 [1536, 69], replicated, may hold values from -0.15625 to 0.15625
- obs_value: float32 [16, 32, 2, 128], P('member', 'space'), may hold values from -6 to 6
- obs_pert: float32 [16, 16, 32, 2, 128], P(None, 'member', 'space'), may hold values from -4 to 4
- obs_index: int32 [16, 32, 2, 128], P('member', 'space'), may hold values from 0 to 1103
- block_list: int32 [16, 32, 4], P('member', 'space'), may hold values from 0 to 17
- list_count: int32 [16, 32], P('member', 'space'), may hold values from 1 to 4, as said below
- gains: bfloat16 [16, 32, 4, 128, 1104], P('member', 'space'), may hold values from -0.375 to 0.375
Outputs:
- increments: float32 [16, 32, 16, 1104], P('member', 'space')
The draws below stay inside these ranges and needn't reach their ends.
Inputs may be any that keep to these rules, and one draw needn't show every extreme that they name: `list_count`: some tile's list has exactly 4 live entries.
All inputs are finite; a program needn't handle non-finite values.
Results may differ from the reference program's by a relative error of at most 0.012.
Values may be sent and summed in bfloat16 or wider, within the bound.
No kernel may reach another device: no remote copies, remote signals or barrier semaphores. Data moves between devices by JAX's collectives and lax.ppermute only.
A program may use at most 64 MiB of HBM per device.

```python
import jax
import jax.numpy as jnp
from jax import lax

D = 1536
HEADS = 24
HS = 32
CH = 69
WIN = 8
LAT = 32
LON_DEV = 8
OB = 128
NBLK = 2
MAXL = 4
SHIFT = 4
HD = 768
ENS = 16
LON = 256
AROWS = 2
ACELLS = 1104
N_MEMBER = 16
N_SPACE = 32


def draw_rel_bias(key, part):
    key = jax.random.fold_in(key, 11)
    keys = jax.random.split(key, 1)
    span = WIN * WIN
    return jax.random.truncated_normal(keys[0], -4.0, 4.0, (HEADS, span, span), jnp.float32)


def draw_list_count(key, part):
    key = jax.random.fold_in(key, 5)
    keys = jax.random.split(key, 2)
    counts = jax.random.randint(keys[0], (N_MEMBER * N_SPACE,), 1, MAXL + 1)
    marked = jax.random.randint(keys[1], (), 0, N_MEMBER * N_SPACE)
    counts = jnp.where(jnp.arange(N_MEMBER * N_SPACE) == marked, MAXL, counts)
    return counts.reshape(N_MEMBER, N_SPACE).astype(jnp.int32)


def plant(values, stream_key, smallest, top_value):
    dims = values.shape
    place = [jax.random.randint(jax.random.fold_in(stream_key, axis), (), 0, dims[axis]) for axis in range(len(dims))]
    values = values.at[tuple(place)].set(smallest)
    longest = dims.index(max(dims))
    place[longest] = (place[longest] + 1) % dims[longest]
    return values.at[tuple(place)].set(top_value)


def block_scale(rng, shape, cuts, low, high):
    def one(dim, shards_of):
        heights = jax.random.uniform(jax.random.fold_in(jax.random.fold_in(rng, 6), dim), (shards_of,), jnp.float32, low / len(cuts), high / len(cuts))
        return jnp.repeat(jnp.exp(heights), shape[dim] // shards_of).reshape((-1,) + (1,) * (len(shape) - dim - 1))

    loudness = one(*cuts[0])
    for cut in cuts[1:]:
        loudness = loudness * one(*cut)
    return loudness


def normal_values(key, shape, width, bound, shards=(), held_as=jnp.bfloat16):
    entries = jax.random.normal(key, shape, jnp.float32) * width
    if len(shards) > 0:
        entries = block_scale(key, shape, shards, -0.22, 0.18) * entries
    return jnp.clip(entries, min=-bound, max=bound).astype(held_as)


def setup_inputs(seed: int = 0) -> dict:
    key_of = jax.random.split(jax.random.key(seed), 13)
    return {
        "tokens": normal_values(key_of[0], (ENS, LAT, LON, D), 1.0, 6.0, ((0, 16), (2, 32))),
        "norm_gain": jnp.clip(1.0 + 0.18 * jax.random.normal(key_of[1], (D,), jnp.float32), 0.1, 1.9),
        "w_qkv": normal_values(key_of[2], (D, 3 * HD), D ** -0.5, 0.15625, ((0, 32),)),
        "w_out": normal_values(key_of[3], (HD, D), HD ** -0.5, 0.21875, ((0, 32),)),
        "rel_bias": draw_rel_bias(jax.random.fold_in(key_of[12], 71), 0),
        "w_decode": normal_values(key_of[5], (D, CH), D ** -0.5, 0.15625),
        "obs_value": normal_values(key_of[6], (N_MEMBER, N_SPACE, NBLK, OB), 1.0, 6.0, ((0, 16), (1, 32)), jnp.float32),
        "obs_pert": normal_values(key_of[7], (ENS, N_MEMBER, N_SPACE, NBLK, OB), 0.5, 4.0, ((1, 16), (2, 32)), jnp.float32),
        "obs_index": plant(jax.random.randint(key_of[8], (N_MEMBER, N_SPACE, NBLK, OB), 0, ACELLS), jax.random.fold_in(key_of[8], 1), 0, ACELLS - 1).astype(jnp.int32),
        "block_list": plant(jax.random.randint(key_of[9], (N_MEMBER, N_SPACE, MAXL), 0, 9 * NBLK), jax.random.fold_in(key_of[9], 1), 0, (9 * NBLK) - 1).astype(jnp.int32),
        "list_count": draw_list_count(jax.random.fold_in(key_of[12], 71), 0),
        "gains": normal_values(key_of[11], (N_MEMBER, N_SPACE, MAXL, OB, ACELLS), (2 * OB) ** -0.5, 0.375, ((0, 16), (1, 32))),
    }


def layer_norm(values, gain_row):
    widened = values.astype(jnp.float32)
    center = lax.optimization_barrier(jnp.mean(widened, axis=-1, keepdims=True))
    spread = lax.optimization_barrier(jnp.mean((widened - center) ** 2, axis=-1, keepdims=True))
    return ((widened - center) * lax.rsqrt(spread + 1e-05) * gain_row).astype(jnp.bfloat16)

def to_windows(array, lat_count, col_count):
    shaped = array.reshape(lat_count // WIN, WIN, col_count // WIN, WIN, HEADS, HS)
    return shaped.transpose(0, 2, 4, 1, 3, 5).reshape(lat_count // WIN, col_count // WIN, HEADS, WIN * WIN, HS)

def from_windows(blocked, lat_count, col_count):
    shaped = blocked.reshape(lat_count // WIN, col_count // WIN, HEADS, WIN, WIN, HS)
    return shaped.transpose(0, 3, 1, 4, 2, 5).reshape(lat_count, col_count, HEADS * HS)

def window_attention(queries, key_part, value_part, rel_bias):
    lat_count, col_count = (queries.shape[0], queries.shape[1])
    query_win = to_windows(queries, lat_count, col_count).astype(jnp.float32)
    key_win = to_windows(key_part, lat_count, col_count).astype(jnp.float32)
    value_win = to_windows(value_part, lat_count, col_count).astype(jnp.float32)
    scores = jnp.einsum('abhqd,abhkd->abhqk', query_win, key_win) * HS ** (-0.5) + rel_bias
    weights = jax.nn.softmax(scores, axis=-1).astype(jnp.bfloat16)
    mixed = jnp.einsum('abhqk,abhkd->abhqd', weights.astype(jnp.float32), value_win).astype(jnp.bfloat16)
    return from_windows(mixed, lat_count, col_count)

def reference(tokens, norm_gain, w_qkv, w_out, rel_bias, w_decode, obs_value, obs_pert, obs_index, block_list, list_count, gains):
    head_width = HEADS * HS

    def member_step(member_grid):
        normed = layer_norm(member_grid, norm_gain).reshape(-1, D)
        projected = jnp.dot(normed, w_qkv, preferred_element_type=jnp.float32).astype(jnp.bfloat16)
        projected = jnp.roll(projected.reshape(LAT, LON, 3 * head_width), -SHIFT, axis=1)
        attended = window_attention(projected[:, :, :head_width], projected[:, :, head_width:2 * head_width], projected[:, :, 2 * head_width:], rel_bias)
        attended = jnp.roll(attended, SHIFT, axis=1).reshape(-1, head_width)
        output_sum = jnp.dot(attended, w_out, preferred_element_type=jnp.float32)
        updated = (member_grid.reshape(-1, D).astype(jnp.float32) + output_sum).astype(jnp.bfloat16)
        return jnp.dot(updated, w_decode, preferred_element_type=jnp.float32).reshape(LAT, LON, CH)
    fields = lax.map(member_step, tokens)
    tiles = fields.reshape(ENS, N_MEMBER, AROWS, N_SPACE, LON_DEV, CH).transpose(1, 3, 0, 2, 4, 5)
    tiles = tiles.reshape(N_MEMBER, N_SPACE, ENS, ACELLS)
    flat_index = jnp.broadcast_to(obs_index.reshape(N_MEMBER, N_SPACE, 1, NBLK * OB), (N_MEMBER, N_SPACE, ENS, NBLK * OB))
    observed = jnp.take_along_axis(tiles, flat_index, axis=3).reshape(N_MEMBER, N_SPACE, ENS, NBLK, OB)
    innovation = obs_value[:, :, None] + obs_pert.transpose(1, 2, 0, 3, 4) - observed
    innovation = innovation.transpose(0, 1, 3, 2, 4)
    wrapped = jnp.concatenate([innovation[:, -1:], innovation, innovation[:, :1]], axis=1)
    padded = jnp.pad(wrapped, ((1, 1), (0, 0), (0, 0), (0, 0), (0, 0)))
    beside_all = jnp.stack([padded[row_off:row_off + N_MEMBER, col_off:col_off + N_SPACE] for row_off in range(3) for col_off in range(3)], axis=2)
    beside_all = beside_all.reshape(N_MEMBER, N_SPACE, 9 * NBLK, ENS, OB)
    selected = jnp.take_along_axis(beside_all, block_list[:, :, :, None, None], axis=2)
    live_mask = (jnp.arange(MAXL)[None, None, :] < list_count[:, :, None]).astype(jnp.float32)
    selected = (selected * live_mask[:, :, :, None, None]).astype(jnp.bfloat16)

    def band_update(band):
        chosen, gain_band = band
        return jnp.einsum('sjmo,sjoc->smc', chosen.astype(jnp.float32), gain_band.astype(jnp.float32))
    return lax.map(band_update, (selected, gains))
```

```python
import jax
import jax.numpy as jnp
import numpy as np
from jax import lax
from jax.experimental import pallas as pl
from jax.experimental.pallas import tpu as pltpu
from jax.sharding import Mesh, PartitionSpec as P

HEADS = 24
HS = 32
WIN = 8
SHIFT = 4
CH = 69
MEMBER = ("zhi", "x")
SPACE = ("zlo", "y", "core")
ROW = ("y", "core")
GROUP_HEADS = 12
GF = GROUP_HEADS * HS
WCOLS = 3 * GF + 128
F32 = jnp.float32
BF16 = jnp.bfloat16
NT = (((1,), (1,)), ((), ()))
VMEM_LIMIT = 48 * 1024 * 1024


def dot(a, b, dims=(((1,), (0,)), ((), ()))):
    return lax.dot_general(a, b, dims, preferred_element_type=F32)


def weights_kernel(group_ref, w_qkv_ref, w_out_ref, w_decode_ref, out_ref):
    for group in range(2):

        @pl.when(group_ref[0] == group)
        def _():
            for part in range(3):
                out_ref[:, part * GF : (part + 1) * GF] = w_qkv_ref[
                    :, (2 * part + group) * GF : (2 * part + group + 1) * GF
                ]

    folded = dot(w_out_ref[...], w_decode_ref[...], NT)
    rows, channels = folded.shape
    wide = jnp.concatenate([folded, jnp.zeros((rows, 128 - channels), F32)], axis=1)
    full = jnp.concatenate([wide, jnp.zeros((out_ref.shape[0] - rows, 128), F32)], axis=0)
    out_ref[:, 3 * GF :] = full.astype(BF16)


def norm_kernel(tokens_ref, halo_ref, gain_ref, w_decode_ref, normed_ref, residual_ref):
    own = tokens_ref[0].astype(F32)
    halo = halo_ref[...].astype(F32)
    features = own.shape[-1]
    halo = halo.reshape(WIN // 2, WIN, features)
    halo = jnp.stack([pltpu.roll(halo, 4, axis=1), halo], axis=1).reshape(WIN, WIN, features)
    spot = lax.broadcasted_iota(jnp.int32, (WIN, WIN, features), 1)
    window = jnp.where(spot < SHIFT, pltpu.roll(own, 4, axis=1), halo).reshape(WIN * WIN, features)
    center = jnp.mean(window, axis=-1, keepdims=True)
    spread = jnp.mean((window - center) ** 2, axis=-1, keepdims=True)
    normed = (window - center) * lax.rsqrt(spread + 1e-05) * gain_ref[...]
    normed_ref[...] = normed.astype(BF16)
    residual = dot(window.astype(BF16), w_decode_ref[...], NT)
    residual_ref[...] = jnp.concatenate(
        [residual, jnp.zeros((WIN * WIN, 128 - CH), F32)], axis=1
    )


def attention_kernel(
    group_ref,
    own_ref,
    mate_ref,
    residual_ref,
    weights_hbm,
    bias_ref,
    value_ref,
    pick_ref,
    both_ref,
    right_ref,
    left_ref,
    weights,
    qkv,
    fields,
    sums,
    sems,
):
    copies = []
    for block in range(16):
        for low in range(2):
            copies.append(
                pltpu.make_async_copy(
                    weights_hbm.at[pl.ds((block * 2 + low) * 48, 48)],
                    weights.at[pl.ds((low * 16 + block) * 48, 48)],
                    sems.at[block * 2 + low],
                )
            )
    for copy in copies:
        copy.start()
    for copy in copies:
        copy.wait()
    for member, source in enumerate((own_ref, mate_ref)):
        for part in range(3):
            lanes = slice(part * GF, (part + 1) * GF)
            qkv[member * 256 : (member + 1) * 256, lanes] = dot(source[...], weights[:, lanes]).astype(BF16)
    first = pl.multiple_of(group_ref[0] * 768, 768)
    folded = jnp.concatenate(
        [
            weights[pl.ds(pl.multiple_of(first + 48 * t, 48), 48), 3 * GF :].astype(F32)[:24]
            for t in range(16)
        ],
        axis=0,
    )
    folded_t = [folded[128 * j : 128 * (j + 1)].T.astype(BF16) for j in range(3)]
    head_of_row = lax.broadcasted_iota(jnp.int32, (256, 128), 0) // 64
    head_of_lane = lax.broadcasted_iota(jnp.int32, (256, 128), 1) // 32
    block_mask = head_of_row == head_of_lane
    lane = lax.broadcasted_iota(jnp.int32, (128, 128), 1)
    zero = jnp.zeros((64, 128), BF16)

    def spread_heads(tile):
        return jnp.where(block_mask, jnp.concatenate([tile] * 4, axis=0), jnp.zeros((256, 128), BF16))

    for pair in range(4):
        row_a, row_b = (128 * pair, 128 * pair + 64)
        total = None
        for j in range(3):
            def part_of(part, row):
                return qkv[row : row + 64, part * GF + 128 * j : part * GF + 128 * (j + 1)]

            query = jnp.concatenate(
                [
                    jnp.concatenate([part_of(0, row_a), zero], axis=1),
                    jnp.concatenate([zero, part_of(0, row_b)], axis=1),
                ],
                axis=0,
            )
            key = jnp.concatenate(
                [spread_heads(part_of(1, row_a)), spread_heads(part_of(1, row_b))], axis=1
            )
            scores = dot(key, query, NT) * HS ** (-0.5) + bias_ref[256 * j : 256 * (j + 1)]
            scores = scores.reshape(4, 64, 128)
            powers = jnp.exp(scores - jnp.max(scores, axis=1, keepdims=True))
            chances = powers * (1.0 / jnp.sum(powers, axis=1, keepdims=True))
            chances = chances.reshape(256, 128).astype(BF16)
            value = jnp.concatenate(
                [
                    dot(folded_t[j], spread_heads(part_of(2, row_a)), NT),
                    dot(folded_t[j], spread_heads(part_of(2, row_b)), NT),
                ],
                axis=0,
            ).astype(BF16)
            term = dot(value, chances)
            total = term if total is None else total + term
        decoded = jnp.where(lane < 64, total[:128], total[128:]).T
        if pair < 2:
            decoded = decoded + residual_ref[128 * pair : 128 * (pair + 1)]
        fields[128 * pair : 128 * (pair + 1)] = decoded
    cell = lax.broadcasted_iota(jnp.int32, (8, 128), 0)
    for tile in range(16):
        for block in range(2):
            row = 2 * tile + block
            for side in range(2):
                channel = jnp.broadcast_to(pick_ref[64 * side + row : 64 * side + row + 1], (8, 128))
                place = jnp.broadcast_to(pick_ref[64 * side + 32 + row : 64 * side + 32 + row + 1], (8, 128))
                for member in range(2):
                    found = None
                    for line in range(2):
                        at = member * 256 + 16 * tile + 8 * line
                        gathered = jnp.take_along_axis(fields[at : at + 8], channel, axis=1)
                        kept = jnp.where(place == cell + 8 * line, gathered, 0.0)
                        found = kept if found is None else found + kept
                    found = -jnp.sum(found, axis=0, keepdims=True)
                    if side == 0 and member == 0:
                        found = found + value_ref[row : row + 1]
                    sums[32 * side + row : 32 * side + row + 1, 128 * member : 128 * (member + 1)] = found
    both = sums[...].astype(BF16)
    both_ref[...] = both
    right_ref[...] = both[:32]
    left_ref[...] = both[32:]


def select_kernel(own_ref, prev_ref, next_ref, second_ref, choice_ref, out_ref):
    table = jnp.concatenate(
        [prev_ref[:32], own_ref[:32], next_ref[...], second_ref[...], prev_ref[32:], own_ref[32:]], axis=0
    )
    table = jnp.concatenate([table[:, :128], table[:, 128:]], axis=0)
    out_ref[...] = dot(choice_ref[...], table).astype(BF16).reshape(16, 8, 128)


def update_kernel(arrived_ref, gains_ref, out_ref):
    row = lax.broadcasted_iota(jnp.int32, (64, 128), 0)
    col = lax.broadcasted_iota(jnp.int32, (64, 128), 1)
    entry, member = (row // 16, row % 16)
    source, pair, source_entry = (col // 8, (col // 4) % 2, col % 4)
    same = (entry == source_entry) & ((source ^ pair) == member)
    gather = jnp.where(same, 1.0, 0.0).astype(BF16)
    chosen = dot(gather, arrived_ref[...].reshape(128, 128)).astype(BF16)
    total = None
    for j in range(4):
        term = dot(chosen[16 * j : 16 * (j + 1)], gains_ref[j], NT)
        total = term if total is None else total + term
    out_ref[...] = total


def shift(x, by):
    peers = lax.axis_size(SPACE)
    return lax.ppermute(x, SPACE, [(i, (i + by) % peers) for i in range(peers)])


def smem():
    return pl.BlockSpec(memory_space=pltpu.SMEM)


def vmem():
    return pl.BlockSpec(memory_space=pltpu.VMEM)


def params():
    return pltpu.CompilerParams(vmem_limit_bytes=VMEM_LIMIT)


def body(
    tokens,
    norm_gain,
    w_qkv,
    w_out,
    rel_bias,
    w_decode,
    obs_value,
    obs_pert,
    obs_index,
    block_list,
    list_count,
    gains,
):
    features = tokens.shape[3]
    group = (lax.axis_index("x") % 2).astype(jnp.int32)
    low = lax.axis_index("zlo")
    w_decode_t = w_decode.T

    rows = pl.pallas_call(
        weights_kernel,
        out_shape=jax.ShapeDtypeStruct((w_qkv.shape[0], WCOLS), BF16),
        in_specs=[smem(), vmem(), vmem(), vmem()],
        out_specs=vmem(),
        compiler_params=params(),
        name="weights",
    )(group.reshape(1), w_qkv, w_out, w_decode_t)
    other_rows = lax.ppermute(rows, "zlo", [(0, 1), (1, 0)])
    both_rows = jnp.where(
        low == 0,
        jnp.concatenate([rows, other_rows], axis=0),
        jnp.concatenate([other_rows, rows], axis=0),
    )
    gathered = lax.all_gather(both_rows, ROW, axis=0, tiled=True)

    left_half = tokens[0, :, :SHIFT].reshape(-1, features)
    halo = shift(left_half, -1)
    normed, residual = pl.pallas_call(
        norm_kernel,
        grid=(4,),
        out_shape=(
            jax.ShapeDtypeStruct((256, features), BF16),
            jax.ShapeDtypeStruct((256, 128), F32),
        ),
        in_specs=[
            pl.BlockSpec((1, WIN, WIN, features), lambda i: (0, i, 0, 0)),
            pl.BlockSpec((WIN * SHIFT, features), lambda i: (i, 0)),
            pl.BlockSpec((1, features), lambda i: (0, 0)),
            pl.BlockSpec(w_decode_t.shape, lambda i: (0, 0)),
        ],
        out_specs=(
            pl.BlockSpec((64, features), lambda i: (i, 0)),
            pl.BlockSpec((64, 128), lambda i: (i, 0)),
        ),
        compiler_params=params(),
        name="norm",
    )(tokens, halo, norm_gain.reshape(1, -1), w_decode_t)
    mate = lax.ppermute(normed, "x", [(0, 1), (1, 0), (2, 3), (3, 2)])

    expected = obs_value[0, 0][None] + obs_pert[:, 0, 0]
    entries = block_list.shape[2]
    lists = jnp.concatenate([block_list[0, 0], list_count[0], jnp.zeros((128 - entries - 1,), jnp.int32)])
    notes = jnp.concatenate([obs_index[0, 0], lists[None]], axis=0).astype(F32)
    outgoing = jnp.concatenate([expected, jnp.broadcast_to(notes[None], (16, 3, 128))], axis=1)
    observed = lax.all_to_all(outgoing, MEMBER, split_axis=0, concat_axis=0, tiled=True)
    expected = observed[:, :2].reshape(32, 128)
    index_f = observed[:, 2:4].reshape(32, 128)
    index_next = shift(index_f, -1).astype(jnp.int32)
    index = index_f.astype(jnp.int32)

    def decode(index, side):
        line, rest = (index // (WIN * CH), index % (WIN * CH))
        column, channel = (rest // CH, rest % CH)
        here = (column >= SHIFT) if side == 0 else (column < SHIFT)
        place = line * WIN + (column + SHIFT) % WIN
        return [channel, jnp.where(here, place, -1)]

    picks = jnp.concatenate(decode(index, 0) + decode(index_next, 1), axis=0)
    meta = observed[:, 4].astype(jnp.int32)
    listed, count = (meta[:, :entries], meta[:, entries : entries + 1])
    tile_row = jnp.arange(16)[:, None] + listed // 6 - 1
    live = (jnp.arange(entries)[None] < count) & (tile_row >= 0) & (tile_row < 16)
    table_row = jnp.where(live, (listed // 2 % 3) * 32 + tile_row * 2 + listed % 2, -1000)
    table_row = (table_row[:, None, :] + 192 * jnp.arange(2)[None, :, None]).reshape(128, 1)
    table_col = jnp.arange(384)[None]
    choice = ((table_col == table_row) | (table_col == table_row + 96)).astype(BF16)

    bias = lax.dynamic_slice_in_dim(rel_bias, group * GROUP_HEADS, GROUP_HEADS, axis=0)
    bias = bias.transpose(0, 2, 1).reshape(GROUP_HEADS * 64, 64)
    bias = jnp.concatenate([bias, bias], axis=1)

    both, right, left = pl.pallas_call(
        attention_kernel,
        out_shape=(
            jax.ShapeDtypeStruct((64, 256), BF16),
            jax.ShapeDtypeStruct((32, 256), BF16),
            jax.ShapeDtypeStruct((32, 256), BF16),
        ),
        in_specs=[
            smem(),
            vmem(),
            vmem(),
            vmem(),
            pl.BlockSpec(memory_space=pl.ANY),
            vmem(),
            vmem(),
            vmem(),
        ],
        out_specs=(vmem(), vmem(), vmem()),
        scratch_shapes=[
            pltpu.VMEM((features, WCOLS), BF16),
            pltpu.VMEM((512, 3 * GF), BF16),
            pltpu.VMEM((512, 128), F32),
            pltpu.VMEM((64, 256), F32),
            pltpu.SemaphoreType.DMA((32,)),
        ],
        compiler_params=params(),
        name="attention",
    )(group.reshape(1), normed, mate, residual, gathered, bias, expected, picks)

    previous, following, second = (shift(both, 1), shift(right, -1), shift(left, 2))
    selected = pl.pallas_call(
        select_kernel,
        out_shape=jax.ShapeDtypeStruct((16, 8, 128), BF16),
        in_specs=[vmem()] * 5,
        out_specs=vmem(),
        compiler_params=params(),
        name="select",
    )(both, previous, following, second, choice)
    arrived = lax.all_to_all(selected, MEMBER, split_axis=0, concat_axis=0, tiled=True)
    gains_t = gains[0, 0].transpose(0, 2, 1)
    increment = pl.pallas_call(
        update_kernel,
        out_shape=jax.ShapeDtypeStruct((16, gains.shape[4]), F32),
        in_specs=[vmem(), vmem()],
        out_specs=vmem(),
        compiler_params=params(),
        name="update",
    )(arrived, gains_t)
    return increment[None, None]


def solution(mesh):
    fine = Mesh(np.asarray(mesh.devices).reshape(4, 4, 2, 8, 2), ("zhi", "x", "zlo", "y", "core"))
    in_specs = (
        P(MEMBER, None, SPACE, None),
        P(),
        P(SPACE, None),
        P(SPACE, None),
        P(),
        P(),
        P(MEMBER, SPACE, None, None),
        P(None, MEMBER, SPACE, None, None),
        P(MEMBER, SPACE, None, None),
        P(MEMBER, SPACE, None),
        P(MEMBER, SPACE),
        P(MEMBER, SPACE, None, None, None),
    )
    out_specs = P(MEMBER, SPACE, None, None)
    return jax.shard_map(body, mesh=fine, in_specs=in_specs, out_specs=out_specs, check_vma=False)
```

```python
import jax
import jax.numpy as jnp
import numpy as np
from jax import lax
from jax.experimental import pallas as pl
from jax.experimental.pallas import tpu as pltpu
from jax.sharding import Mesh, PartitionSpec as P

HEADS = 24
HS = 32
WIN = 8
SHIFT = 4
MAXL = 4
CH = 69
MEMBER = ("zhi", "x")
SPACE = ("zlo", "y", "core")
ROW = ("y", "core")
GROUP_HEADS = 12
GF = GROUP_HEADS * HS
WCOLS = 3 * GF + 128
F32 = jnp.float32
BF16 = jnp.bfloat16
NT = (((1,), (1,)), ((), ()))
VMEM_LIMIT = 8 * 1024 * 1024


def dot(a, b, dims=(((1,), (0,)), ((), ()))):
    return lax.dot_general(a, b, dims, preferred_element_type=F32)


def weights_kernel(group_ref, w_qkv_ref, w_out_ref, w_decode_ref, out_ref):
    for group in range(2):

        @pl.when(group_ref[0] == group)
        def _():
            for part in range(3):
                out_ref[:, part * GF : (part + 1) * GF] = w_qkv_ref[
                    :, (2 * part + group) * GF : (2 * part + group + 1) * GF
                ]

    folded = dot(w_out_ref[...], w_decode_ref[...], NT)
    rows, channels = folded.shape
    wide = jnp.concatenate([folded, jnp.zeros((rows, 128 - channels), F32)], axis=1)
    full = jnp.concatenate([wide, jnp.zeros((out_ref.shape[0] - rows, 128), F32)], axis=0)
    out_ref[:, 3 * GF :] = full.astype(BF16)


def edge_kernel(tokens_ref, index_ref, out_ref):
    tile = tokens_ref[0].astype(F32)
    lines, _, features = tile.shape
    tile = tile.reshape(lines // 2, 2, WIN, features)
    spot = lax.broadcasted_iota(jnp.int32, (lines // 2, WIN, features), 1)
    packed = jnp.where(spot < SHIFT, tile[:, 0], pltpu.roll(tile[:, 1], 4, axis=1))
    rows = lines * SHIFT
    out_ref[:rows] = packed.reshape(rows, features).astype(BF16)
    index = index_ref[...]
    upper = (index // 32).astype(F32)
    lower = (index % 32).astype(F32)
    wide = jnp.concatenate(
        [upper[:1], upper[1:], lower[:1], lower[1:], jnp.zeros((1, features - 512), F32)], axis=1
    )
    out_ref[rows:] = jnp.broadcast_to(wide, (16, features)).astype(BF16)


def bias_kernel(group_ref, rel_bias_ref, out_ref):
    for head in range(GROUP_HEADS):
        turned = rel_bias_ref[head].T
        out_ref[64 * head : 64 * (head + 1)] = jnp.concatenate([turned, turned], axis=1)


def norm_kernel(
    list_ref,
    count_ref,
    tokens_ref,
    halo_ref,
    extra_ref,
    gain_ref,
    w_decode_ref,
    value_ref,
    pert_ref,
    index_ref,
    normed_ref,
    residual_ref,
    notes_ref,
):
    @pl.when(pl.program_id(0) == 0)
    def _():
        parts = extra_ref[:8].astype(F32)
        following = [parts[:1, 128 * b : 128 * (b + 1)] * 32.0 + parts[:1, 256 + 128 * b : 384 + 128 * b] for b in range(2)]
        lane = lax.broadcasted_iota(jnp.int32, (1, 128), 1)
        listed = jnp.where(lane == MAXL, count_ref[0], 0)
        for j in range(MAXL):
            listed = jnp.where(lane == j, list_ref[j], listed)
        same = jnp.concatenate(
            [index_ref[...].astype(F32)] + following + [listed.astype(F32), jnp.zeros((1, 128), F32)], axis=0
        )
        for member in range(16):
            notes_ref[member] = jnp.concatenate([value_ref[...] + pert_ref[member], same], axis=0)

    own = tokens_ref[0].astype(F32)
    halo = halo_ref[...].astype(F32)
    features = own.shape[-1]
    halo = halo.reshape(WIN // 2, WIN, features)
    halo = jnp.stack([pltpu.roll(halo, 4, axis=1), halo], axis=1).reshape(WIN, WIN, features)
    spot = lax.broadcasted_iota(jnp.int32, (WIN, WIN, features), 1)
    window = jnp.where(spot < SHIFT, pltpu.roll(own, 4, axis=1), halo).reshape(WIN * WIN, features)
    center = jnp.mean(window, axis=-1, keepdims=True)
    spread = jnp.mean((window - center) ** 2, axis=-1, keepdims=True)
    normed = (window - center) * lax.rsqrt(spread + 1e-05) * gain_ref[...]
    normed_ref[...] = normed.astype(BF16)
    residual = dot(window.astype(BF16), w_decode_ref[...], NT)
    residual_ref[...] = jnp.concatenate(
        [residual, jnp.zeros((WIN * WIN, 128 - CH), F32)], axis=1
    )


def attention_kernel(
    group_ref,
    starts_ref,
    own_ref,
    mate_ref,
    residual_ref,
    blocks,
    bias_ref,
    value_ref,
    pick_ref,
    both_ref,
    right_ref,
    left_ref,
    weights,
    qkv,
    fields,
    sums,
    sems,
):
    copies = []
    for i, block in enumerate(blocks):
        for half in range(2):
            for low in range(2):
                start = pl.multiple_of(starts_ref[2 * i + half] + 768 * low, 48)
                copies.append(
                    pltpu.make_async_copy(
                        block.at[pl.ds(96 * half + 48 * low, 48)],
                        weights.at[pl.ds(start, 48)],
                        sems.at[4 * i + 2 * half + low],
                    )
                )
    for copy in copies:
        copy.start()
    for copy in copies:
        copy.wait()
    for member, source in enumerate((own_ref, mate_ref)):
        for part in range(3):
            lanes = slice(part * GF, (part + 1) * GF)
            qkv[member * 256 : (member + 1) * 256, lanes] = dot(source[...], weights[:, lanes]).astype(BF16)
    first = pl.multiple_of(group_ref[0] * 768, 768)
    folded = jnp.concatenate(
        [
            weights[pl.ds(pl.multiple_of(first + 48 * t, 48), 48), 3 * GF :].astype(F32)[:24]
            for t in range(16)
        ],
        axis=0,
    )
    folded_t = [folded[128 * j : 128 * (j + 1)].T.astype(BF16) for j in range(3)]
    head_of_row = lax.broadcasted_iota(jnp.int32, (256, 128), 0) // 64
    head_of_lane = lax.broadcasted_iota(jnp.int32, (256, 128), 1) // 32
    block_mask = head_of_row == head_of_lane
    lane = lax.broadcasted_iota(jnp.int32, (128, 128), 1)
    zero = jnp.zeros((64, 128), BF16)

    def spread_heads(tile):
        return jnp.where(block_mask, jnp.concatenate([tile] * 4, axis=0), jnp.zeros((256, 128), BF16))

    for pair in range(4):
        row_a, row_b = (128 * pair, 128 * pair + 64)
        total = None
        for j in range(3):
            def part_of(part, row):
                return qkv[row : row + 64, part * GF + 128 * j : part * GF + 128 * (j + 1)]

            query = jnp.concatenate(
                [
                    jnp.concatenate([part_of(0, row_a), zero], axis=1),
                    jnp.concatenate([zero, part_of(0, row_b)], axis=1),
                ],
                axis=0,
            )
            key = jnp.concatenate(
                [spread_heads(part_of(1, row_a)), spread_heads(part_of(1, row_b))], axis=1
            )
            scores = dot(key, query, NT) * HS ** (-0.5) + bias_ref[256 * j : 256 * (j + 1)]
            scores = scores.reshape(4, 64, 128)
            powers = jnp.exp(scores - jnp.max(scores, axis=1, keepdims=True))
            chances = powers * (1.0 / jnp.sum(powers, axis=1, keepdims=True))
            chances = chances.reshape(256, 128).astype(BF16)
            value = jnp.concatenate(
                [
                    dot(folded_t[j], spread_heads(part_of(2, row_a)), NT),
                    dot(folded_t[j], spread_heads(part_of(2, row_b)), NT),
                ],
                axis=0,
            ).astype(BF16)
            term = dot(value, chances)
            total = term if total is None else total + term
        decoded = jnp.where(lane < 64, total[:128], total[128:]).T
        if pair < 2:
            decoded = decoded + residual_ref[128 * pair : 128 * (pair + 1)]
        fields[128 * pair : 128 * (pair + 1)] = decoded
    cell = lax.broadcasted_iota(jnp.int32, (8, 128), 0)
    for tile in range(16):
        for block in range(2):
            row = 2 * tile + block
            for side in range(2):
                channel = jnp.broadcast_to(pick_ref[64 * side + row : 64 * side + row + 1], (8, 128))
                place = jnp.broadcast_to(pick_ref[64 * side + 32 + row : 64 * side + 32 + row + 1], (8, 128))
                for member in range(2):
                    found = None
                    for line in range(2):
                        at = member * 256 + 16 * tile + 8 * line
                        gathered = jnp.take_along_axis(fields[at : at + 8], channel, axis=1)
                        kept = jnp.where(place == cell + 8 * line, gathered, 0.0)
                        found = kept if found is None else found + kept
                    found = -jnp.sum(found, axis=0, keepdims=True)
                    if side == 0 and member == 0:
                        found = found + value_ref[row : row + 1]
                    sums[32 * side + row : 32 * side + row + 1, 128 * member : 128 * (member + 1)] = found
    both = sums[...].astype(BF16)
    both_ref[...] = both
    right_ref[...] = both[:32]
    left_ref[...] = both[32:]


def select_kernel(own_ref, prev_ref, next_ref, second_ref, choice_ref, out_ref):
    table = jnp.concatenate(
        [prev_ref[:32], own_ref[:32], next_ref[...], second_ref[...], prev_ref[32:], own_ref[32:]], axis=0
    )
    table = jnp.concatenate([table[:, :128], table[:, 128:]], axis=0)
    out_ref[...] = dot(choice_ref[...], table).astype(BF16).reshape(16, 8, 128)


def update_kernel(arrived_ref, gains_ref, out_ref):
    row = lax.broadcasted_iota(jnp.int32, (64, 128), 0)
    col = lax.broadcasted_iota(jnp.int32, (64, 128), 1)
    entry, member = (row // 16, row % 16)
    source, pair, source_entry = (col // 8, (col // 4) % 2, col % 4)
    same = (entry == source_entry) & ((source ^ pair) == member)
    gather = jnp.where(same, 1.0, 0.0).astype(BF16)
    chosen = dot(gather, arrived_ref[...].reshape(128, 128)).astype(BF16)
    total = None
    for j in range(4):
        term = dot(chosen[16 * j : 16 * (j + 1)], gains_ref[j], NT)
        total = term if total is None else total + term
    out_ref[...] = total


def shift(x, by):
    peers = lax.axis_size(SPACE)
    return lax.ppermute(x, SPACE, [(i, (i + by) % peers) for i in range(peers)])


def swap_pairs(first):
    pairs = []
    for y in range(8):
        for core in range(2):
            odd_pairing = (core == 0) != first
            other = (y ^ 1) if not odd_pairing else ((y + 1) % 8 if y % 2 else (y - 1) % 8)
            pairs.append((2 * y + core, 2 * other + core))
    return pairs


def swap_index(y, core, first):
    odd_pairing = (core == 0) != first
    even = jnp.where(y % 2 == 1, y - 1, y + 1)
    odd = jnp.where(y % 2 == 1, (y + 1) % 8, (y + 7) % 8)
    return jnp.where(odd_pairing, odd, even)


def core_swap(x):
    return lax.ppermute(x, "core", [(0, 1), (1, 0)])


def block_starts(y, core):
    starts = []
    for of_core in (core, 1 - core):
        places = [y, swap_index(y, of_core, True)]
        for chain in ([False], [True, False], [False, True, False]):
            at = y
            for step in chain:
                at = swap_index(at, of_core, step)
            places += [at, swap_index(at, of_core, True)]
        starts += [place * 96 + of_core * 48 for place in places]
    return jnp.stack(starts).astype(jnp.int32)


def smem():
    return pl.BlockSpec(memory_space=pltpu.SMEM)


def vmem():
    return pl.BlockSpec(memory_space=pltpu.VMEM)


def params(limit=VMEM_LIMIT):
    return pltpu.CompilerParams(vmem_limit_bytes=limit)


def body(
    tokens,
    norm_gain,
    w_qkv,
    w_out,
    rel_bias,
    w_decode,
    obs_value,
    obs_pert,
    obs_index,
    block_list,
    list_count,
    gains,
):
    features = tokens.shape[3]
    group = (lax.axis_index("x") % 2).astype(jnp.int32)
    w_decode_t = w_decode.T

    rows = pl.pallas_call(
        weights_kernel,
        out_shape=jax.ShapeDtypeStruct((w_qkv.shape[0], WCOLS), BF16),
        in_specs=[smem(), vmem(), vmem(), vmem()],
        out_specs=vmem(),
        compiler_params=params(),
        name="weights",
    )(group.reshape(1), w_qkv, w_out, w_decode_t)
    core, low, y = (lax.axis_index("core"), lax.axis_index("zlo"), lax.axis_index("y"))
    far = lax.ppermute(rows, "zlo", [(0, 1), (1, 0)])
    block = jnp.where(
        low == 0, jnp.concatenate([rows, far], axis=0), jnp.concatenate([far, rows], axis=0)
    )
    first, second = (swap_pairs(True), swap_pairs(False))
    near = lax.ppermute(block, ROW, first)

    edge = pl.pallas_call(
        edge_kernel,
        out_shape=jax.ShapeDtypeStruct((32 * SHIFT + 16, features), BF16),
        in_specs=[vmem(), vmem()],
        out_specs=vmem(),
        compiler_params=params(),
        name="edge",
    )(tokens, obs_index[0, 0])
    halo = shift(edge, -1)
    near, halo = lax.optimization_barrier((near, halo))
    held = [jnp.concatenate([block, near], axis=0)]
    held.append(lax.ppermute(held[0], ROW, second))
    normed, residual, notes = pl.pallas_call(
        norm_kernel,
        grid=(4,),
        out_shape=(
            jax.ShapeDtypeStruct((256, features), BF16),
            jax.ShapeDtypeStruct((256, 128), F32),
            jax.ShapeDtypeStruct((16, 8, 128), F32),
        ),
        in_specs=[
            smem(),
            smem(),
            pl.BlockSpec((1, WIN, WIN, features), lambda i: (0, i, 0, 0)),
            pl.BlockSpec((WIN * SHIFT, features), lambda i: (i, 0)),
            pl.BlockSpec((16, features), lambda i: (8, 0)),
            pl.BlockSpec((1, features), lambda i: (0, 0)),
            pl.BlockSpec(w_decode_t.shape, lambda i: (0, 0)),
            pl.BlockSpec((2, 128), lambda i: (0, 0)),
            pl.BlockSpec((16, 2, 128), lambda i: (0, 0, 0)),
            pl.BlockSpec((2, 128), lambda i: (0, 0)),
        ],
        out_specs=(
            pl.BlockSpec((64, features), lambda i: (i, 0)),
            pl.BlockSpec((64, 128), lambda i: (i, 0)),
            pl.BlockSpec((16, 8, 128), lambda i: (0, 0, 0)),
        ),
        compiler_params=params(),
        name="norm",
    )(
        block_list[0, 0],
        list_count[0],
        tokens,
        halo,
        halo,
        norm_gain.reshape(1, -1),
        w_decode_t,
        obs_value[0, 0],
        obs_pert[:, 0, 0],
        obs_index[0, 0],
    )
    mate = lax.ppermute(normed, "x", [(0, 1), (1, 0), (2, 3), (3, 2)])
    held[1], _ = lax.optimization_barrier((held[1], normed))
    held.append(lax.ppermute(held[1], ROW, first))
    swapped = [core_swap(held[0]), core_swap(held[1])]
    held[2], *swapped = lax.optimization_barrier((held[2], *swapped))
    held.append(lax.ppermute(held[2], ROW, second))
    last, mate = lax.optimization_barrier((held[3], mate))
    swapped += [core_swap(held[2]), core_swap(last)]
    blocks = held + swapped
    starts = block_starts(y, core)

    notes, _ = lax.optimization_barrier((notes, blocks[6]))
    observed = lax.all_to_all(notes, MEMBER, split_axis=0, concat_axis=0, tiled=True)
    entries = block_list.shape[2]
    expected = observed[:, :2].reshape(32, 128)
    index = observed[:, 2:4].reshape(32, 128).astype(jnp.int32)
    index_next = observed[:, 4:6].reshape(32, 128).astype(jnp.int32)

    def decode(index, side):
        line, rest = (index // (WIN * CH), index % (WIN * CH))
        column, channel = (rest // CH, rest % CH)
        here = (column >= SHIFT) if side == 0 else (column < SHIFT)
        place = line * WIN + (column + SHIFT) % WIN
        return [channel, jnp.where(here, place, -1)]

    picks = jnp.concatenate(decode(index, 0) + decode(index_next, 1), axis=0)
    meta = observed[:, 6].astype(jnp.int32)
    listed, count = (meta[:, :entries], meta[:, entries : entries + 1])
    tile_row = jnp.arange(16)[:, None] + listed // 6 - 1
    live = (jnp.arange(entries)[None] < count) & (tile_row >= 0) & (tile_row < 16)
    table_row = jnp.where(live, (listed // 2 % 3) * 32 + tile_row * 2 + listed % 2, -1000)
    table_row = (table_row[:, None, :] + 192 * jnp.arange(2)[None, :, None]).reshape(128, 1)
    table_col = jnp.arange(384)[None]
    choice = ((table_col == table_row) | (table_col == table_row + 96)).astype(BF16)

    bias = pl.pallas_call(
        bias_kernel,
        grid_spec=pltpu.PrefetchScalarGridSpec(
            num_scalar_prefetch=1,
            grid=(1,),
            in_specs=[pl.BlockSpec((GROUP_HEADS, 64, 64), lambda i, group: (group[0], 0, 0))],
            out_specs=pl.BlockSpec((GROUP_HEADS * 64, 128), lambda i, group: (0, 0)),
        ),
        out_shape=jax.ShapeDtypeStruct((GROUP_HEADS * 64, 128), F32),
        compiler_params=params(),
        name="bias",
    )(group.reshape(1), rel_bias)

    both, right, left = pl.pallas_call(
        attention_kernel,
        out_shape=(
            jax.ShapeDtypeStruct((64, 256), BF16),
            jax.ShapeDtypeStruct((32, 256), BF16),
            jax.ShapeDtypeStruct((32, 256), BF16),
        ),
        in_specs=[
            smem(),
            smem(),
            vmem(),
            vmem(),
            vmem(),
            [pl.BlockSpec(memory_space=pl.ANY)] * 8,
            vmem(),
            vmem(),
            vmem(),
        ],
        out_specs=(vmem(), vmem(), vmem()),
        scratch_shapes=[
            pltpu.VMEM((features, WCOLS), BF16),
            pltpu.VMEM((512, 3 * GF), BF16),
            pltpu.VMEM((512, 128), F32),
            pltpu.VMEM((64, 256), F32),
            pltpu.SemaphoreType.DMA((32,)),
        ],
        compiler_params=params(61 * 1024 * 1024),
        name="attention",
    )(group.reshape(1), starts, normed, mate, residual, blocks, bias, expected, picks)

    previous, following, second = (shift(both, 1), shift(right, -1), shift(left, 2))
    selected = pl.pallas_call(
        select_kernel,
        out_shape=jax.ShapeDtypeStruct((16, 8, 128), BF16),
        in_specs=[vmem()] * 5,
        out_specs=vmem(),
        compiler_params=params(),
        name="select",
    )(both, previous, following, second, choice)
    arrived = lax.all_to_all(selected, MEMBER, split_axis=0, concat_axis=0, tiled=True)
    gains_t = gains[0, 0].transpose(0, 2, 1)
    increment = pl.pallas_call(
        update_kernel,
        out_shape=jax.ShapeDtypeStruct((16, gains.shape[4]), F32),
        in_specs=[vmem(), vmem()],
        out_specs=vmem(),
        compiler_params=params(),
        name="update",
    )(arrived, gains_t)
    return increment[None, None]


def solution(mesh):
    fine = Mesh(np.asarray(mesh.devices).reshape(4, 4, 2, 8, 2), ("zhi", "x", "zlo", "y", "core"))
    in_specs = (
        P(MEMBER, None, SPACE, None),
        P(),
        P(SPACE, None),
        P(SPACE, None),
        P(),
        P(),
        P(MEMBER, SPACE, None, None),
        P(None, MEMBER, SPACE, None, None),
        P(MEMBER, SPACE, None, None),
        P(MEMBER, SPACE, None),
        P(MEMBER, SPACE),
        P(MEMBER, SPACE, None, None, None),
    )
    out_specs = P(MEMBER, SPACE, None, None)
    return jax.shard_map(body, mesh=fine, in_specs=in_specs, out_specs=out_specs, check_vma=False)
```

```python
import jax
import jax.numpy as jnp
import numpy as np
from jax import lax
from jax.experimental import pallas as pl
from jax.experimental.pallas import tpu as pltpu
from jax.sharding import Mesh, PartitionSpec as P

HEADS = 24
HS = 32
WIN = 8
SHIFT = 4
MAXL = 4
CH = 69
MEMBER = ("zhi", "x")
SPACE = ("zlo", "y", "core")
ROW = ("y", "core")
GROUP_HEADS = 12
GF = GROUP_HEADS * HS
WCOLS = 3 * GF + 128
F32 = jnp.float32
BF16 = jnp.bfloat16
NT = (((1,), (1,)), ((), ()))
VMEM_LIMIT = 8 * 1024 * 1024


def dot(a, b, dims=(((1,), (0,)), ((), ()))):
    return lax.dot_general(a, b, dims, preferred_element_type=F32)


def weights_kernel(group_ref, w_qkv_ref, w_out_ref, w_decode_ref, out_ref):
    for group in range(2):

        @pl.when(group_ref[0] == group)
        def _():
            for part in range(3):
                out_ref[:, part * GF : (part + 1) * GF] = w_qkv_ref[
                    :, (2 * part + group) * GF : (2 * part + group + 1) * GF
                ]

    folded = dot(w_out_ref[...], w_decode_ref[...], NT)
    rows, channels = folded.shape
    wide = jnp.concatenate([folded, jnp.zeros((rows, 128 - channels), F32)], axis=1)
    full = jnp.concatenate([wide, jnp.zeros((out_ref.shape[0] - rows, 128), F32)], axis=0)
    out_ref[:, 3 * GF :] = full.astype(BF16)


def edge_kernel(tokens_ref, index_ref, out_ref):
    tile = tokens_ref[0].astype(F32)
    lines, _, features = tile.shape
    tile = tile.reshape(lines // 2, 2, WIN, features)
    spot = lax.broadcasted_iota(jnp.int32, (lines // 2, WIN, features), 1)
    packed = jnp.where(spot < SHIFT, tile[:, 0], pltpu.roll(tile[:, 1], 4, axis=1))
    rows = lines * SHIFT
    out_ref[:rows] = packed.reshape(rows, features).astype(BF16)
    index = index_ref[...]
    upper = (index // 32).astype(F32)
    lower = (index % 32).astype(F32)
    wide = jnp.concatenate(
        [upper[:1], upper[1:], lower[:1], lower[1:], jnp.zeros((1, features - 512), F32)], axis=1
    )
    out_ref[rows:] = jnp.broadcast_to(wide, (16, features)).astype(BF16)


def bias_kernel(group_ref, rel_bias_ref, out_ref):
    for head in range(GROUP_HEADS):
        turned = rel_bias_ref[head].T
        out_ref[64 * head : 64 * (head + 1)] = jnp.concatenate([turned, turned], axis=1)


def norm_kernel(
    list_ref,
    count_ref,
    tokens_ref,
    halo_ref,
    extra_ref,
    gain_ref,
    w_decode_ref,
    value_ref,
    pert_ref,
    index_ref,
    normed_ref,
    residual_ref,
    notes_ref,
):
    @pl.when(pl.program_id(0) == 0)
    def _():
        parts = extra_ref[:8].astype(F32)
        following = [parts[:1, 128 * b : 128 * (b + 1)] * 32.0 + parts[:1, 256 + 128 * b : 384 + 128 * b] for b in range(2)]
        lane = lax.broadcasted_iota(jnp.int32, (1, 128), 1)
        listed = jnp.where(lane == MAXL, count_ref[0], 0)
        for j in range(MAXL):
            listed = jnp.where(lane == j, list_ref[j], listed)
        same = jnp.concatenate(
            [index_ref[...].astype(F32)] + following + [listed.astype(F32), jnp.zeros((1, 128), F32)], axis=0
        )
        for member in range(16):
            notes_ref[member] = jnp.concatenate([value_ref[...] + pert_ref[member], same], axis=0)

    own = tokens_ref[0].astype(F32)
    halo = halo_ref[...].astype(F32)
    features = own.shape[-1]
    halo = halo.reshape(WIN // 2, WIN, features)
    halo = jnp.stack([pltpu.roll(halo, 4, axis=1), halo], axis=1).reshape(WIN, WIN, features)
    spot = lax.broadcasted_iota(jnp.int32, (WIN, WIN, features), 1)
    window = jnp.where(spot < SHIFT, pltpu.roll(own, 4, axis=1), halo).reshape(WIN * WIN, features)
    center = jnp.mean(window, axis=-1, keepdims=True)
    spread = jnp.mean((window - center) ** 2, axis=-1, keepdims=True)
    normed = (window - center) * lax.rsqrt(spread + 1e-05) * gain_ref[...]
    normed_ref[...] = normed.astype(BF16)
    residual = dot(window.astype(BF16), w_decode_ref[...], NT)
    residual_ref[...] = jnp.concatenate(
        [residual, jnp.zeros((WIN * WIN, 128 - CH), F32)], axis=1
    )


def attention_kernel(
    group_ref,
    starts_ref,
    own_ref,
    mate_ref,
    residual_ref,
    blocks,
    bias_ref,
    observed_ref,
    both_ref,
    right_ref,
    left_ref,
    weights,
    qkv,
    fields,
    sums,
    sems,
):
    copies = []
    for part, lanes in enumerate((slice(0, GF), slice(GF, 2 * GF), slice(2 * GF, WCOLS))):
        for i, block in enumerate(blocks):
            for half in range(2):
                for low in range(2):
                    start = pl.multiple_of(starts_ref[2 * i + half] + 768 * low, 48)
                    copies.append(
                        pltpu.make_async_copy(
                            block.at[pl.ds(96 * half + 48 * low, 48), lanes],
                            weights.at[pl.ds(start, 48), lanes],
                            sems.at[part, 4 * i + 2 * half + low],
                        )
                    )
    for copy in copies:
        copy.start()
    for part in range(3):
        for copy in copies[32 * part : 32 * (part + 1)]:
            copy.wait()
        lanes = slice(part * GF, (part + 1) * GF)
        for member, source in enumerate((own_ref, mate_ref)):
            qkv[member * 256 : (member + 1) * 256, lanes] = dot(source[...], weights[:, lanes]).astype(BF16)
    first = pl.multiple_of(group_ref[0] * 768, 768)
    folded = jnp.concatenate(
        [
            weights[pl.ds(pl.multiple_of(first + 48 * t, 48), 48), 3 * GF :].astype(F32)[:24]
            for t in range(16)
        ],
        axis=0,
    )
    folded_t = [folded[128 * j : 128 * (j + 1)].T.astype(BF16) for j in range(3)]
    head_of_row = lax.broadcasted_iota(jnp.int32, (256, 128), 0) // 64
    head_of_lane = lax.broadcasted_iota(jnp.int32, (256, 128), 1) // 32
    block_mask = head_of_row == head_of_lane
    lane = lax.broadcasted_iota(jnp.int32, (128, 128), 1)
    zero = jnp.zeros((64, 128), BF16)

    def spread_heads(tile):
        return jnp.where(block_mask, jnp.concatenate([tile] * 4, axis=0), jnp.zeros((256, 128), BF16))

    for pair in range(4):
        row_a, row_b = (128 * pair, 128 * pair + 64)
        total = None
        for j in range(3):
            def part_of(part, row):
                return qkv[row : row + 64, part * GF + 128 * j : part * GF + 128 * (j + 1)]

            query = jnp.concatenate(
                [
                    jnp.concatenate([part_of(0, row_a), zero], axis=1),
                    jnp.concatenate([zero, part_of(0, row_b)], axis=1),
                ],
                axis=0,
            )
            key = jnp.concatenate(
                [spread_heads(part_of(1, row_a)), spread_heads(part_of(1, row_b))], axis=1
            )
            scores = dot(key, query, NT) * HS ** (-0.5) + bias_ref[256 * j : 256 * (j + 1)]
            scores = scores.reshape(4, 64, 128)
            powers = jnp.exp(scores - jnp.max(scores, axis=1, keepdims=True))
            chances = powers * (1.0 / jnp.sum(powers, axis=1, keepdims=True))
            chances = chances.reshape(256, 128).astype(BF16)
            value = jnp.concatenate(
                [
                    dot(folded_t[j], spread_heads(part_of(2, row_a)), NT),
                    dot(folded_t[j], spread_heads(part_of(2, row_b)), NT),
                ],
                axis=0,
            ).astype(BF16)
            term = dot(value, chances)
            total = term if total is None else total + term
        decoded = jnp.where(lane < 64, total[:128], total[128:]).T
        if pair < 2:
            decoded = decoded + residual_ref[128 * pair : 128 * (pair + 1)]
        fields[128 * pair : 128 * (pair + 1)] = decoded
    cell = lax.broadcasted_iota(jnp.int32, (8, 128), 0)
    for tile in range(16):
        for block in range(2):
            for side in range(2):
                at = 2 + 2 * side + block
                code = jnp.broadcast_to(observed_ref[tile, at : at + 1].astype(jnp.int32), (8, 128))
                channel, place = (code & 127, code >> 7)
                for member in range(2):
                    found = None
                    for half in range(2):
                        row = member * 256 + 16 * tile + 8 * half
                        gathered = jnp.take_along_axis(fields[row : row + 8], channel, axis=1)
                        kept = jnp.where(place == cell + 8 * half, gathered, 0.0)
                        found = kept if found is None else found + kept
                    found = -jnp.sum(found, axis=0, keepdims=True)
                    if side == 0 and member == 0:
                        found = found + observed_ref[tile, block : block + 1]
                    row = 32 * side + 2 * tile + block
                    sums[row : row + 1, 128 * member : 128 * (member + 1)] = found
    both = sums[...].astype(BF16)
    both_ref[...] = both
    right_ref[...] = both[:32]
    left_ref[...] = both[32:]


def decode_kernel(observed_ref, out_ref):
    index = observed_ref[...]
    line = jnp.where(index >= WIN * CH, 1.0, 0.0)
    rest = index - line * (WIN * CH)
    column = jnp.floor((rest + 0.5) * (1.0 / CH))
    channel = rest - column * CH
    side = lax.broadcasted_iota(jnp.int32, index.shape, 1)
    late = column >= SHIFT
    place = line * WIN + jnp.where(late, column - SHIFT, column + SHIFT)
    inside = late == (side < 4)
    place = jnp.where(inside, place, 64.0)
    out_ref[...] = jnp.where(side < 2, index, place * 128.0 + channel)


def select_kernel(chosen_ref, own_ref, prev_ref, next_ref, second_ref, out_ref, table, picked):
    for place, part in enumerate(
        (prev_ref[:32], own_ref[:32], next_ref[...], second_ref[...], prev_ref[32:], own_ref[32:])
    ):
        table[32 * place : 32 * (place + 1)] = part.astype(F32)
    table[192:200] = jnp.zeros((8, 256), F32)
    table[288:296] = jnp.zeros((8, 256), F32)
    for band in range(16):
        for j in range(MAXL):
            row = chosen_ref[MAXL * band + j]
            found = table[pl.ds(row, 1)] + table[pl.ds(row + 96, 1)]
            for member in range(2):
                to = MAXL * member + j
                picked[band, to : to + 1] = found[:, 128 * member : 128 * (member + 1)]
    out_ref[...] = picked[...].astype(BF16)


def update_kernel(arrived_ref, gains_ref, out_ref):
    row = lax.broadcasted_iota(jnp.int32, (64, 128), 0)
    col = lax.broadcasted_iota(jnp.int32, (64, 128), 1)
    entry, member = (row // 16, row % 16)
    source, pair, source_entry = (col // 8, (col // 4) % 2, col % 4)
    same = (entry == source_entry) & ((source ^ pair) == member)
    gather = jnp.where(same, 1.0, 0.0).astype(BF16)
    chosen = dot(gather, arrived_ref[...].reshape(128, 128)).astype(BF16)
    total = None
    for j in range(4):
        term = dot(chosen[16 * j : 16 * (j + 1)], gains_ref[j], NT)
        total = term if total is None else total + term
    out_ref[...] = total


def shift(x, by):
    peers = lax.axis_size(SPACE)
    return lax.ppermute(x, SPACE, [(i, (i + by) % peers) for i in range(peers)])


def swap_pairs(first):
    pairs = []
    for y in range(8):
        for core in range(2):
            odd_pairing = (core == 0) != first
            other = (y ^ 1) if not odd_pairing else ((y + 1) % 8 if y % 2 else (y - 1) % 8)
            pairs.append((2 * y + core, 2 * other + core))
    return pairs


def swap_index(y, core, first):
    odd_pairing = (core == 0) != first
    even = jnp.where(y % 2 == 1, y - 1, y + 1)
    odd = jnp.where(y % 2 == 1, (y + 1) % 8, (y + 7) % 8)
    return jnp.where(odd_pairing, odd, even)


def core_swap(x):
    return lax.ppermute(x, "core", [(0, 1), (1, 0)])


def block_starts(y, core):
    starts = []
    for of_core in (core, 1 - core):
        places = [y, swap_index(y, of_core, True)]
        for chain in ([False], [True, False], [False, True, False]):
            at = y
            for step in chain:
                at = swap_index(at, of_core, step)
            places += [at, swap_index(at, of_core, True)]
        starts += [place * 96 + of_core * 48 for place in places]
    return jnp.stack(starts).astype(jnp.int32)


def smem():
    return pl.BlockSpec(memory_space=pltpu.SMEM)


def vmem():
    return pl.BlockSpec(memory_space=pltpu.VMEM)


def params(limit=VMEM_LIMIT):
    return pltpu.CompilerParams(vmem_limit_bytes=limit)


def body(
    tokens,
    norm_gain,
    w_qkv,
    w_out,
    rel_bias,
    w_decode,
    obs_value,
    obs_pert,
    obs_index,
    block_list,
    list_count,
    gains,
):
    features = tokens.shape[3]
    group = (lax.axis_index("x") % 2).astype(jnp.int32)
    w_decode_t = w_decode.T

    rows = pl.pallas_call(
        weights_kernel,
        out_shape=jax.ShapeDtypeStruct((w_qkv.shape[0], WCOLS), BF16),
        in_specs=[smem(), vmem(), vmem(), vmem()],
        out_specs=vmem(),
        compiler_params=params(63 * 1024 * 1024),
        name="weights",
    )(group.reshape(1), w_qkv, w_out, w_decode_t)
    core, low, y = (lax.axis_index("core"), lax.axis_index("zlo"), lax.axis_index("y"))
    far = lax.ppermute(rows, "zlo", [(0, 1), (1, 0)])
    block = jnp.where(
        low == 0, jnp.concatenate([rows, far], axis=0), jnp.concatenate([far, rows], axis=0)
    )
    first, second = (swap_pairs(True), swap_pairs(False))
    near = lax.ppermute(block, ROW, first)

    edge = pl.pallas_call(
        edge_kernel,
        out_shape=jax.ShapeDtypeStruct((32 * SHIFT + 16, features), BF16),
        in_specs=[vmem(), vmem()],
        out_specs=vmem(),
        compiler_params=params(),
        name="edge",
    )(tokens, obs_index[0, 0])
    halo = shift(edge, -1)
    near, halo = lax.optimization_barrier((near, halo))
    held = [jnp.concatenate([block, near], axis=0)]
    held.append(lax.ppermute(held[0], ROW, second))
    normed, residual, notes = pl.pallas_call(
        norm_kernel,
        grid=(4,),
        out_shape=(
            jax.ShapeDtypeStruct((256, features), BF16),
            jax.ShapeDtypeStruct((256, 128), F32),
            jax.ShapeDtypeStruct((16, 8, 128), F32),
        ),
        in_specs=[
            smem(),
            smem(),
            pl.BlockSpec((1, WIN, WIN, features), lambda i: (0, i, 0, 0)),
            pl.BlockSpec((WIN * SHIFT, features), lambda i: (i, 0)),
            pl.BlockSpec((16, features), lambda i: (8, 0)),
            pl.BlockSpec((1, features), lambda i: (0, 0)),
            pl.BlockSpec(w_decode_t.shape, lambda i: (0, 0)),
            pl.BlockSpec((2, 128), lambda i: (0, 0)),
            pl.BlockSpec((16, 2, 128), lambda i: (0, 0, 0)),
            pl.BlockSpec((2, 128), lambda i: (0, 0)),
        ],
        out_specs=(
            pl.BlockSpec((64, features), lambda i: (i, 0)),
            pl.BlockSpec((64, 128), lambda i: (i, 0)),
            pl.BlockSpec((16, 8, 128), lambda i: (0, 0, 0)),
        ),
        compiler_params=params(),
        name="norm",
    )(
        block_list[0, 0],
        list_count[0],
        tokens,
        halo,
        halo,
        norm_gain.reshape(1, -1),
        w_decode_t,
        obs_value[0, 0],
        obs_pert[:, 0, 0],
        obs_index[0, 0],
    )
    mate = lax.ppermute(normed, "x", [(0, 1), (1, 0), (2, 3), (3, 2)])
    bias = pl.pallas_call(
        bias_kernel,
        grid_spec=pltpu.PrefetchScalarGridSpec(
            num_scalar_prefetch=1,
            grid=(1,),
            in_specs=[pl.BlockSpec((GROUP_HEADS, 64, 64), lambda i, group: (group[0], 0, 0))],
            out_specs=pl.BlockSpec((GROUP_HEADS * 64, 128), lambda i, group: (0, 0)),
        ),
        out_shape=jax.ShapeDtypeStruct((GROUP_HEADS * 64, 128), F32),
        compiler_params=params(),
        name="bias",
    )(group.reshape(1), rel_bias)
    starts = block_starts(y, core)
    held[1], bias, starts, _ = lax.optimization_barrier((held[1], bias, starts, normed))
    held.append(lax.ppermute(held[1], ROW, first))
    swapped = [core_swap(held[0]), core_swap(held[1])]
    held[2], *swapped = lax.optimization_barrier((held[2], *swapped))
    held.append(lax.ppermute(held[2], ROW, second))
    swapped.append(core_swap(held[2]))

    notes, _ = lax.optimization_barrier((notes, held[2]))
    observed = lax.all_to_all(notes, MEMBER, split_axis=0, concat_axis=0, tiled=True)
    entries = pl.pallas_call(
        decode_kernel,
        out_shape=jax.ShapeDtypeStruct((16, 8, 128), F32),
        in_specs=[vmem()],
        out_specs=vmem(),
        cost_estimate=pl.CostEstimate(flops=4 * 10**9, bytes_accessed=10**6, transcendentals=0),
        compiler_params=params(),
        name="decode",
    )(observed)
    last, mate = lax.optimization_barrier((held[3], mate))
    swapped.append(core_swap(last))
    blocks = held + swapped

    meta = observed[:, 6].astype(jnp.int32)
    listed, count = (meta[:, :MAXL], meta[:, MAXL : MAXL + 1])
    band = jnp.arange(16)[:, None] + listed // 6 - 1
    live = (jnp.arange(MAXL)[None] < count) & (band >= 0) & (band < 16)
    chosen = jnp.where(live, (listed // 2 % 3) * 32 + band * 2 + listed % 2, 192).reshape(16 * MAXL)

    both, right, left = pl.pallas_call(
        attention_kernel,
        out_shape=(
            jax.ShapeDtypeStruct((64, 256), BF16),
            jax.ShapeDtypeStruct((32, 256), BF16),
            jax.ShapeDtypeStruct((32, 256), BF16),
        ),
        in_specs=[
            smem(),
            smem(),
            vmem(),
            vmem(),
            vmem(),
            [pl.BlockSpec(memory_space=pl.ANY)] * 8,
            vmem(),
            vmem(),
        ],
        out_specs=(vmem(), vmem(), vmem()),
        scratch_shapes=[
            pltpu.VMEM((features, WCOLS), BF16),
            pltpu.VMEM((512, 3 * GF), BF16),
            pltpu.VMEM((512, 128), F32),
            pltpu.VMEM((64, 256), F32),
            pltpu.SemaphoreType.DMA((3, 32)),
        ],
        compiler_params=params(48 * 1024 * 1024),
        name="attention",
    )(group.reshape(1), starts, normed, mate, residual, blocks, bias, entries)

    previous, following, second = (shift(both, 1), shift(right, -1), shift(left, 2))
    selected = pl.pallas_call(
        select_kernel,
        out_shape=jax.ShapeDtypeStruct((16, 8, 128), BF16),
        in_specs=[smem()] + [vmem()] * 4,
        out_specs=vmem(),
        scratch_shapes=[pltpu.VMEM((296, 256), F32), pltpu.VMEM((16, 8, 128), F32)],
        compiler_params=params(),
        name="select",
    )(chosen, both, previous, following, second)
    arrived = lax.all_to_all(selected, MEMBER, split_axis=0, concat_axis=0, tiled=True)
    gains_t = gains[0, 0].transpose(0, 2, 1)
    increment = pl.pallas_call(
        update_kernel,
        out_shape=jax.ShapeDtypeStruct((16, gains.shape[4]), F32),
        in_specs=[vmem(), vmem()],
        out_specs=vmem(),
        compiler_params=params(),
        name="update",
    )(arrived, gains_t)
    return increment[None, None]


def solution(mesh):
    fine = Mesh(np.asarray(mesh.devices).reshape(4, 4, 2, 8, 2), ("zhi", "x", "zlo", "y", "core"))
    in_specs = (
        P(MEMBER, None, SPACE, None),
        P(),
        P(SPACE, None),
        P(SPACE, None),
        P(),
        P(),
        P(MEMBER, SPACE, None, None),
        P(None, MEMBER, SPACE, None, None),
        P(MEMBER, SPACE, None, None),
        P(MEMBER, SPACE, None),
        P(MEMBER, SPACE),
        P(MEMBER, SPACE, None, None, None),
    )
    out_specs = P(MEMBER, SPACE, None, None)
    return jax.shard_map(body, mesh=fine, in_specs=in_specs, out_specs=out_specs, check_vma=False)
```

```python
import jax
import jax.numpy as jnp
import numpy as np
from jax import lax
from jax.experimental import pallas as pl
from jax.experimental.pallas import tpu as pltpu
from jax.sharding import Mesh, PartitionSpec as P

HEADS = 24
HS = 32
WIN = 8
SHIFT = 4
MAXL = 4
CH = 69
MEMBER = ("zhi", "x")
SPACE = ("zlo", "y", "core")
ROW = ("y", "core")
GROUP_HEADS = 12
GF = GROUP_HEADS * HS
WCOLS = 3 * GF + 128
F32 = jnp.float32
BF16 = jnp.bfloat16
NT = (((1,), (1,)), ((), ()))
VMEM_LIMIT = 8 * 1024 * 1024


def dot(a, b, dims=(((1,), (0,)), ((), ()))):
    return lax.dot_general(a, b, dims, preferred_element_type=F32)


def weights_kernel(group_ref, w_qkv_ref, w_out_ref, w_decode_ref, out_ref):
    for group in range(2):

        @pl.when(group_ref[0] == group)
        def _():
            for part in range(3):
                out_ref[:, part * GF : (part + 1) * GF] = w_qkv_ref[
                    :, (2 * part + group) * GF : (2 * part + group + 1) * GF
                ]

    folded = dot(w_out_ref[...], w_decode_ref[...], NT)
    rows, channels = folded.shape
    wide = jnp.concatenate([folded, jnp.zeros((rows, 128 - channels), F32)], axis=1)
    full = jnp.concatenate([wide, jnp.zeros((out_ref.shape[0] - rows, 128), F32)], axis=0)
    out_ref[:, 3 * GF :] = full.astype(BF16)


def edge_kernel(tokens_ref, index_ref, out_ref):
    tile = tokens_ref[0].astype(F32)
    lines, _, features = tile.shape
    tile = tile.reshape(lines // 2, 2, WIN, features)
    spot = lax.broadcasted_iota(jnp.int32, (lines // 2, WIN, features), 1)
    packed = jnp.where(spot < SHIFT, tile[:, 0], pltpu.roll(tile[:, 1], 4, axis=1))
    rows = lines * SHIFT
    out_ref[:rows] = packed.reshape(rows, features).astype(BF16)
    index = index_ref[...]
    upper = (index // 32).astype(F32)
    lower = (index % 32).astype(F32)
    wide = jnp.concatenate(
        [upper[:1], upper[1:], lower[:1], lower[1:], jnp.zeros((1, features - 512), F32)], axis=1
    )
    out_ref[rows:] = jnp.broadcast_to(wide, (16, features)).astype(BF16)


def bias_kernel(group_ref, rel_bias_ref, out_ref):
    for head in range(GROUP_HEADS):
        turned = rel_bias_ref[head].T
        out_ref[64 * head : 64 * (head + 1)] = jnp.concatenate([turned, turned], axis=1)


def norm_kernel(
    list_ref,
    count_ref,
    tokens_ref,
    halo_ref,
    extra_ref,
    gain_ref,
    w_decode_ref,
    value_ref,
    pert_ref,
    index_ref,
    normed_ref,
    residual_ref,
    notes_ref,
):
    @pl.when(pl.program_id(0) == 0)
    def _():
        parts = extra_ref[:8].astype(F32)
        following = [parts[:1, 128 * b : 128 * (b + 1)] * 32.0 + parts[:1, 256 + 128 * b : 384 + 128 * b] for b in range(2)]
        lane = lax.broadcasted_iota(jnp.int32, (1, 128), 1)
        listed = jnp.where(lane == MAXL, count_ref[0], 0)
        for j in range(MAXL):
            listed = jnp.where(lane == j, list_ref[j], listed)
        same = jnp.concatenate(
            [index_ref[...].astype(F32)] + following + [listed.astype(F32), jnp.zeros((1, 128), F32)], axis=0
        )
        for member in range(16):
            notes_ref[member] = jnp.concatenate([value_ref[...] + pert_ref[member], same], axis=0)

    own = tokens_ref[0].astype(F32)
    halo = halo_ref[...].astype(F32)
    features = own.shape[-1]
    halo = halo.reshape(WIN // 2, WIN, features)
    halo = jnp.stack([pltpu.roll(halo, 4, axis=1), halo], axis=1).reshape(WIN, WIN, features)
    spot = lax.broadcasted_iota(jnp.int32, (WIN, WIN, features), 1)
    window = jnp.where(spot < SHIFT, pltpu.roll(own, 4, axis=1), halo).reshape(WIN * WIN, features)
    center = jnp.mean(window, axis=-1, keepdims=True)
    spread = jnp.mean((window - center) ** 2, axis=-1, keepdims=True)
    normed = (window - center) * lax.rsqrt(spread + 1e-05) * gain_ref[...]
    normed_ref[...] = normed.astype(BF16)
    residual = dot(window.astype(BF16), w_decode_ref[...], NT)
    residual_ref[...] = jnp.concatenate(
        [residual, jnp.zeros((WIN * WIN, 128 - CH), F32)], axis=1
    )


def attention_kernel(
    group_ref,
    starts_ref,
    own_ref,
    mate_ref,
    residual_ref,
    blocks,
    bias_ref,
    observed_ref,
    both_ref,
    right_ref,
    left_ref,
    weights,
    qkv,
    fields,
    sums,
):
    for i, block in enumerate(blocks):
        for half in range(2):
            for low in range(2):
                start = pl.multiple_of(starts_ref[2 * i + half] + 768 * low, 48)
                row = 96 * half + 48 * low
                weights[pl.ds(start, 48), :] = block[row : row + 48]
    for part in range(3):
        lanes = slice(part * GF, (part + 1) * GF)
        for member, source in enumerate((own_ref, mate_ref)):
            qkv[member * 256 : (member + 1) * 256, lanes] = dot(source[...], weights[:, lanes]).astype(BF16)
    first = pl.multiple_of(group_ref[0] * 768, 768)
    folded = jnp.concatenate(
        [
            weights[pl.ds(pl.multiple_of(first + 48 * t, 48), 48), 3 * GF :].astype(F32)[:24]
            for t in range(16)
        ],
        axis=0,
    )
    folded_t = [folded[128 * j : 128 * (j + 1)].T.astype(BF16) for j in range(3)]
    head_of_row = lax.broadcasted_iota(jnp.int32, (256, 128), 0) // 64
    head_of_lane = lax.broadcasted_iota(jnp.int32, (256, 128), 1) // 32
    block_mask = head_of_row == head_of_lane
    lane = lax.broadcasted_iota(jnp.int32, (128, 128), 1)
    zero = jnp.zeros((64, 128), BF16)

    def spread_heads(tile):
        return jnp.where(block_mask, jnp.concatenate([tile] * 4, axis=0), jnp.zeros((256, 128), BF16))

    for pair in range(4):
        row_a, row_b = (128 * pair, 128 * pair + 64)
        total = None
        for j in range(3):
            def part_of(part, row):
                return qkv[row : row + 64, part * GF + 128 * j : part * GF + 128 * (j + 1)]

            query = jnp.concatenate(
                [
                    jnp.concatenate([part_of(0, row_a), zero], axis=1),
                    jnp.concatenate([zero, part_of(0, row_b)], axis=1),
                ],
                axis=0,
            )
            key = jnp.concatenate(
                [spread_heads(part_of(1, row_a)), spread_heads(part_of(1, row_b))], axis=1
            )
            scores = dot(key, query, NT) * HS ** (-0.5) + bias_ref[256 * j : 256 * (j + 1)]
            scores = scores.reshape(4, 64, 128)
            powers = jnp.exp(scores - jnp.max(scores, axis=1, keepdims=True))
            chances = powers * (1.0 / jnp.sum(powers, axis=1, keepdims=True))
            chances = chances.reshape(256, 128).astype(BF16)
            value = jnp.concatenate(
                [
                    dot(folded_t[j], spread_heads(part_of(2, row_a)), NT),
                    dot(folded_t[j], spread_heads(part_of(2, row_b)), NT),
                ],
                axis=0,
            ).astype(BF16)
            term = dot(value, chances)
            total = term if total is None else total + term
        decoded = jnp.where(lane < 64, total[:128], total[128:]).T
        if pair < 2:
            decoded = decoded + residual_ref[128 * pair : 128 * (pair + 1)]
        fields[128 * pair : 128 * (pair + 1)] = decoded
    cell = lax.broadcasted_iota(jnp.int32, (8, 128), 0)
    for tile in range(16):
        for block in range(2):
            for side in range(2):
                at = 2 + 2 * side + block
                code = jnp.broadcast_to(observed_ref[tile, at : at + 1].astype(jnp.int32), (8, 128))
                channel, place = (code & 127, code >> 7)
                for member in range(2):
                    found = None
                    for half in range(2):
                        row = member * 256 + 16 * tile + 8 * half
                        gathered = jnp.take_along_axis(fields[row : row + 8], channel, axis=1)
                        kept = jnp.where(place == cell + 8 * half, gathered, 0.0)
                        found = kept if found is None else found + kept
                    found = -jnp.sum(found, axis=0, keepdims=True)
                    if side == 0 and member == 0:
                        found = found + observed_ref[tile, block : block + 1]
                    row = 32 * side + 2 * tile + block
                    sums[row : row + 1, 128 * member : 128 * (member + 1)] = found
    both = sums[...].astype(BF16)
    both_ref[...] = both
    right_ref[...] = both[:32]
    left_ref[...] = both[32:]


def decode_kernel(observed_ref, out_ref):
    index = observed_ref[...]
    line = jnp.where(index >= WIN * CH, 1.0, 0.0)
    rest = index - line * (WIN * CH)
    column = jnp.floor((rest + 0.5) * (1.0 / CH))
    channel = rest - column * CH
    side = lax.broadcasted_iota(jnp.int32, index.shape, 1)
    late = column >= SHIFT
    place = line * WIN + jnp.where(late, column - SHIFT, column + SHIFT)
    inside = late == (side < 4)
    place = jnp.where(inside, place, 64.0)
    out_ref[...] = jnp.where(side < 2, index, place * 128.0 + channel)


def select_kernel(chosen_ref, own_ref, prev_ref, next_ref, second_ref, out_ref, table, picked):
    for place, part in enumerate(
        (prev_ref[:32], own_ref[:32], next_ref[...], second_ref[...], prev_ref[32:], own_ref[32:])
    ):
        table[32 * place : 32 * (place + 1)] = part.astype(F32)
    table[192:200] = jnp.zeros((8, 256), F32)
    table[288:296] = jnp.zeros((8, 256), F32)
    for band in range(16):
        for j in range(MAXL):
            row = chosen_ref[MAXL * band + j]
            found = table[pl.ds(row, 1)] + table[pl.ds(row + 96, 1)]
            for member in range(2):
                to = MAXL * member + j
                picked[band, to : to + 1] = found[:, 128 * member : 128 * (member + 1)]
    out_ref[...] = picked[...].astype(BF16)


def update_kernel(arrived_ref, gains_ref, out_ref):
    row = lax.broadcasted_iota(jnp.int32, (64, 128), 0)
    col = lax.broadcasted_iota(jnp.int32, (64, 128), 1)
    entry, member = (row // 16, row % 16)
    source, pair, source_entry = (col // 8, (col // 4) % 2, col % 4)
    same = (entry == source_entry) & ((source ^ pair) == member)
    gather = jnp.where(same, 1.0, 0.0).astype(BF16)
    chosen = dot(gather, arrived_ref[...].reshape(128, 128)).astype(BF16)
    total = None
    for j in range(4):
        term = dot(chosen[16 * j : 16 * (j + 1)], gains_ref[j], NT)
        total = term if total is None else total + term
    out_ref[...] = total


def shift(x, by):
    peers = lax.axis_size(SPACE)
    return lax.ppermute(x, SPACE, [(i, (i + by) % peers) for i in range(peers)])


def swap_pairs(first):
    pairs = []
    for y in range(8):
        for core in range(2):
            odd_pairing = (core == 0) != first
            other = (y ^ 1) if not odd_pairing else ((y + 1) % 8 if y % 2 else (y - 1) % 8)
            pairs.append((2 * y + core, 2 * other + core))
    return pairs


def swap_index(y, core, first):
    odd_pairing = (core == 0) != first
    even = jnp.where(y % 2 == 1, y - 1, y + 1)
    odd = jnp.where(y % 2 == 1, (y + 1) % 8, (y + 7) % 8)
    return jnp.where(odd_pairing, odd, even)


def core_swap(x):
    return lax.ppermute(x, "core", [(0, 1), (1, 0)])


def block_starts(y, core):
    starts = []
    for of_core in (core, 1 - core):
        places = [y, swap_index(y, of_core, True)]
        for chain in ([False], [True, False], [False, True, False]):
            at = y
            for step in chain:
                at = swap_index(at, of_core, step)
            places += [at, swap_index(at, of_core, True)]
        starts += [place * 96 + of_core * 48 for place in places]
    return jnp.stack(starts).astype(jnp.int32)


def smem():
    return pl.BlockSpec(memory_space=pltpu.SMEM)


def vmem():
    return pl.BlockSpec(memory_space=pltpu.VMEM)


def params(limit=VMEM_LIMIT):
    return pltpu.CompilerParams(vmem_limit_bytes=limit)


def body(
    tokens,
    norm_gain,
    w_qkv,
    w_out,
    rel_bias,
    w_decode,
    obs_value,
    obs_pert,
    obs_index,
    block_list,
    list_count,
    gains,
):
    features = tokens.shape[3]
    group = (lax.axis_index("x") % 2).astype(jnp.int32)
    w_decode_t = w_decode.T

    rows = pl.pallas_call(
        weights_kernel,
        out_shape=jax.ShapeDtypeStruct((w_qkv.shape[0], WCOLS), BF16),
        in_specs=[smem(), vmem(), vmem(), vmem()],
        out_specs=vmem(),
        compiler_params=params(63 * 1024 * 1024),
        name="weights",
    )(group.reshape(1), w_qkv, w_out, w_decode_t)
    core, low, y = (lax.axis_index("core"), lax.axis_index("zlo"), lax.axis_index("y"))
    far = lax.ppermute(rows, "zlo", [(0, 1), (1, 0)])
    block = jnp.where(
        low == 0, jnp.concatenate([rows, far], axis=0), jnp.concatenate([far, rows], axis=0)
    )
    first, second = (swap_pairs(True), swap_pairs(False))
    near = lax.ppermute(block, ROW, first)

    edge = pl.pallas_call(
        edge_kernel,
        out_shape=jax.ShapeDtypeStruct((32 * SHIFT + 16, features), BF16),
        in_specs=[vmem(), vmem()],
        out_specs=vmem(),
        compiler_params=params(),
        name="edge",
    )(tokens, obs_index[0, 0])
    halo = shift(edge, -1)
    near, halo = lax.optimization_barrier((near, halo))
    held = [jnp.concatenate([block, near], axis=0)]
    held.append(lax.ppermute(held[0], ROW, second))
    normed, residual, notes = pl.pallas_call(
        norm_kernel,
        grid=(4,),
        out_shape=(
            jax.ShapeDtypeStruct((256, features), BF16),
            jax.ShapeDtypeStruct((256, 128), F32),
            jax.ShapeDtypeStruct((16, 8, 128), F32),
        ),
        in_specs=[
            smem(),
            smem(),
            pl.BlockSpec((1, WIN, WIN, features), lambda i: (0, i, 0, 0)),
            pl.BlockSpec((WIN * SHIFT, features), lambda i: (i, 0)),
            pl.BlockSpec((16, features), lambda i: (8, 0)),
            pl.BlockSpec((1, features), lambda i: (0, 0)),
            pl.BlockSpec(w_decode_t.shape, lambda i: (0, 0)),
            pl.BlockSpec((2, 128), lambda i: (0, 0)),
            pl.BlockSpec((16, 2, 128), lambda i: (0, 0, 0)),
            pl.BlockSpec((2, 128), lambda i: (0, 0)),
        ],
        out_specs=(
            pl.BlockSpec((64, features), lambda i: (i, 0)),
            pl.BlockSpec((64, 128), lambda i: (i, 0)),
            pl.BlockSpec((16, 8, 128), lambda i: (0, 0, 0)),
        ),
        compiler_params=params(),
        name="norm",
    )(
        block_list[0, 0],
        list_count[0],
        tokens,
        halo,
        halo,
        norm_gain.reshape(1, -1),
        w_decode_t,
        obs_value[0, 0],
        obs_pert[:, 0, 0],
        obs_index[0, 0],
    )
    mate = lax.ppermute(normed, "x", [(0, 1), (1, 0), (2, 3), (3, 2)])
    bias = pl.pallas_call(
        bias_kernel,
        grid_spec=pltpu.PrefetchScalarGridSpec(
            num_scalar_prefetch=1,
            grid=(1,),
            in_specs=[pl.BlockSpec((GROUP_HEADS, 64, 64), lambda i, group: (group[0], 0, 0))],
            out_specs=pl.BlockSpec((GROUP_HEADS * 64, 128), lambda i, group: (0, 0)),
        ),
        out_shape=jax.ShapeDtypeStruct((GROUP_HEADS * 64, 128), F32),
        compiler_params=params(),
        name="bias",
    )(group.reshape(1), rel_bias)
    starts = block_starts(y, core)
    held[1], bias, starts, _ = lax.optimization_barrier((held[1], bias, starts, normed))
    held.append(lax.ppermute(held[1], ROW, first))
    swapped = [core_swap(held[0]), core_swap(held[1])]
    held[2], swapped[0] = lax.optimization_barrier((held[2], swapped[0]))
    held.append(lax.ppermute(held[2], ROW, second))
    swapped.append(core_swap(held[2]))

    notes, _ = lax.optimization_barrier((notes, held[2]))
    observed = lax.all_to_all(notes, MEMBER, split_axis=0, concat_axis=0, tiled=True)
    entries = pl.pallas_call(
        decode_kernel,
        out_shape=jax.ShapeDtypeStruct((16, 8, 128), F32),
        in_specs=[vmem()],
        out_specs=vmem(),
        cost_estimate=pl.CostEstimate(flops=4 * 10**9, bytes_accessed=10**6, transcendentals=0),
        compiler_params=params(),
        name="decode",
    )(observed)
    last, mate, swapped[1] = lax.optimization_barrier((held[3], mate, swapped[1]))
    swapped.append(core_swap(last))
    blocks = held + swapped

    meta = observed[:, 6].astype(jnp.int32)
    listed, count = (meta[:, :MAXL], meta[:, MAXL : MAXL + 1])
    band = jnp.arange(16)[:, None] + listed // 6 - 1
    live = (jnp.arange(MAXL)[None] < count) & (band >= 0) & (band < 16)
    chosen = jnp.where(live, (listed // 2 % 3) * 32 + band * 2 + listed % 2, 192).reshape(16 * MAXL)

    both, right, left = pl.pallas_call(
        attention_kernel,
        out_shape=(
            jax.ShapeDtypeStruct((64, 256), BF16),
            jax.ShapeDtypeStruct((32, 256), BF16),
            jax.ShapeDtypeStruct((32, 256), BF16),
        ),
        in_specs=[
            smem(),
            smem(),
            vmem(),
            vmem(),
            vmem(),
            [vmem()] * 8,
            vmem(),
            vmem(),
        ],
        out_specs=(vmem(), vmem(), vmem()),
        scratch_shapes=[
            pltpu.VMEM((features, WCOLS), BF16),
            pltpu.VMEM((512, 3 * GF), BF16),
            pltpu.VMEM((512, 128), F32),
            pltpu.VMEM((64, 256), F32),
        ],
        compiler_params=params(48 * 1024 * 1024),
        name="attention",
    )(group.reshape(1), starts, normed, mate, residual, blocks, bias, entries)

    previous, following, second = (shift(both, 1), shift(right, -1), shift(left, 2))
    selected = pl.pallas_call(
        select_kernel,
        out_shape=jax.ShapeDtypeStruct((16, 8, 128), BF16),
        in_specs=[smem()] + [vmem()] * 4,
        out_specs=vmem(),
        scratch_shapes=[pltpu.VMEM((296, 256), F32), pltpu.VMEM((16, 8, 128), F32)],
        compiler_params=params(),
        name="select",
    )(chosen, both, previous, following, second)
    arrived = lax.all_to_all(selected, MEMBER, split_axis=0, concat_axis=0, tiled=True)
    gains_t = gains[0, 0].transpose(0, 2, 1)
    increment = pl.pallas_call(
        update_kernel,
        out_shape=jax.ShapeDtypeStruct((16, gains.shape[4]), F32),
        in_specs=[vmem(), vmem()],
        out_specs=vmem(),
        compiler_params=params(),
        name="update",
    )(arrived, gains_t)
    return increment[None, None]


def solution(mesh):
    fine = Mesh(np.asarray(mesh.devices).reshape(4, 4, 2, 8, 2), ("zhi", "x", "zlo", "y", "core"))
    in_specs = (
        P(MEMBER, None, SPACE, None),
        P(),
        P(SPACE, None),
        P(SPACE, None),
        P(),
        P(),
        P(MEMBER, SPACE, None, None),
        P(None, MEMBER, SPACE, None, None),
        P(MEMBER, SPACE, None, None),
        P(MEMBER, SPACE, None),
        P(MEMBER, SPACE),
        P(MEMBER, SPACE, None, None, None),
    )
    out_specs = P(MEMBER, SPACE, None, None)
    return jax.shard_map(body, mesh=fine, in_specs=in_specs, out_specs=out_specs, check_vma=False)
```

```python
import jax
import jax.numpy as jnp
import numpy as np
from jax import lax
from jax.experimental import pallas as pl
from jax.experimental.pallas import tpu as pltpu
from jax.sharding import Mesh, PartitionSpec as P

HEADS = 24
HS = 32
WIN = 8
SHIFT = 4
MAXL = 4
CH = 69
MEMBER = ("zhi", "x")
SPACE = ("zlo", "y", "core")
ROW = ("y", "core")
GROUP_HEADS = 12
GF = GROUP_HEADS * HS
WCOLS = 3 * GF + 128
F32 = jnp.float32
BF16 = jnp.bfloat16
NT = (((1,), (1,)), ((), ()))
VMEM_LIMIT = 8 * 1024 * 1024


def dot(a, b, dims=(((1,), (0,)), ((), ()))):
    return lax.dot_general(a, b, dims, preferred_element_type=F32)


def weights_kernel(group_ref, w_qkv_ref, w_out_ref, w_decode_ref, out_ref):
    for group in range(2):

        @pl.when(group_ref[0] == group)
        def _():
            for part in range(3):
                out_ref[:, part * GF : (part + 1) * GF] = w_qkv_ref[
                    :, (2 * part + group) * GF : (2 * part + group + 1) * GF
                ]

    folded = dot(w_out_ref[...], w_decode_ref[...], NT)
    rows, channels = folded.shape
    wide = jnp.concatenate([folded, jnp.zeros((rows, 128 - channels), F32)], axis=1)
    full = jnp.concatenate([wide, jnp.zeros((out_ref.shape[0] - rows, 128), F32)], axis=0)
    out_ref[:, 3 * GF :] = full.astype(BF16)


def edge_kernel(tokens_ref, index_ref, out_ref):
    tile = tokens_ref[0].astype(F32)
    lines, _, features = tile.shape
    tile = tile.reshape(lines // 2, 2, WIN, features)
    spot = lax.broadcasted_iota(jnp.int32, (lines // 2, WIN, features), 1)
    packed = jnp.where(spot < SHIFT, tile[:, 0], pltpu.roll(tile[:, 1], 4, axis=1))
    rows = lines * SHIFT
    out_ref[:rows] = packed.reshape(rows, features).astype(BF16)
    index = index_ref[...]
    upper = (index // 32).astype(F32)
    lower = (index % 32).astype(F32)
    wide = jnp.concatenate(
        [upper[:1], upper[1:], lower[:1], lower[1:], jnp.zeros((1, features - 512), F32)], axis=1
    )
    out_ref[rows:] = jnp.broadcast_to(wide, (16, features)).astype(BF16)


def bias_kernel(group_ref, rel_bias_ref, out_ref):
    for head in range(GROUP_HEADS):
        turned = rel_bias_ref[head].T
        out_ref[64 * head : 64 * (head + 1)] = jnp.concatenate([turned, turned], axis=1)


def norm_window(tokens_ref, halo_ref, gain_ref):
    own = tokens_ref[0].astype(F32)
    halo = halo_ref[...].astype(F32)
    features = own.shape[-1]
    halo = halo.reshape(WIN // 2, WIN, features)
    halo = jnp.stack([pltpu.roll(halo, 4, axis=1), halo], axis=1).reshape(WIN, WIN, features)
    spot = lax.broadcasted_iota(jnp.int32, (WIN, WIN, features), 1)
    window = jnp.where(spot < SHIFT, pltpu.roll(own, 4, axis=1), halo).reshape(WIN * WIN, features)
    center = jnp.mean(window, axis=-1, keepdims=True)
    spread = jnp.mean((window - center) ** 2, axis=-1, keepdims=True)
    normed = (window - center) * lax.rsqrt(spread + 1e-05) * gain_ref[...]
    return window, normed.astype(BF16)


def own_kernel(tokens_ref, halo_ref, gain_ref, w_decode_ref, normed_ref, residual_ref):
    window, normed_ref[...] = norm_window(tokens_ref, halo_ref, gain_ref)
    residual = dot(window.astype(BF16), w_decode_ref[...], NT)
    residual_ref[...] = jnp.concatenate(
        [residual, jnp.zeros((WIN * WIN, 128 - CH), F32)], axis=1
    )


def norm_kernel(
    list_ref,
    count_ref,
    tokens_ref,
    halo_ref,
    extra_ref,
    gain_ref,
    value_ref,
    pert_ref,
    index_ref,
    normed_ref,
    notes_ref,
):
    @pl.when(pl.program_id(0) == 0)
    def _():
        parts = extra_ref[:8].astype(F32)
        following = [parts[:1, 128 * b : 128 * (b + 1)] * 32.0 + parts[:1, 256 + 128 * b : 384 + 128 * b] for b in range(2)]
        lane = lax.broadcasted_iota(jnp.int32, (1, 128), 1)
        listed = jnp.where(lane == MAXL, count_ref[0], 0)
        for j in range(MAXL):
            listed = jnp.where(lane == j, list_ref[j], listed)
        same = jnp.concatenate(
            [index_ref[...].astype(F32)] + following + [listed.astype(F32), jnp.zeros((1, 128), F32)], axis=0
        )
        for member in range(16):
            notes_ref[member] = jnp.concatenate([value_ref[...] + pert_ref[member], same], axis=0)

    normed_ref[...] = norm_window(tokens_ref, halo_ref, gain_ref)[1]


def attention_kernel(
    group_ref,
    starts_ref,
    own_ref,
    mate_ref,
    residual_ref,
    blocks,
    bias_ref,
    observed_ref,
    both_ref,
    right_ref,
    left_ref,
    weights,
    qkv,
    fields,
    sums,
):
    for i, block in enumerate(blocks):
        for half in range(2):
            for low in range(2):
                start = pl.multiple_of(starts_ref[2 * i + half] + 768 * low, 48)
                row = 96 * half + 48 * low
                weights[pl.ds(start, 48), :] = block[row : row + 48]
    for part in range(3):
        lanes = slice(part * GF, (part + 1) * GF)
        for member, source in enumerate((own_ref, mate_ref)):
            qkv[member * 256 : (member + 1) * 256, lanes] = dot(source[...], weights[:, lanes]).astype(BF16)
    first = pl.multiple_of(group_ref[0] * 768, 768)
    folded = jnp.concatenate(
        [
            weights[pl.ds(pl.multiple_of(first + 48 * t, 48), 48), 3 * GF :].astype(F32)[:24]
            for t in range(16)
        ],
        axis=0,
    )
    folded_t = [folded[128 * j : 128 * (j + 1)].T.astype(BF16) for j in range(3)]
    head_of_row = lax.broadcasted_iota(jnp.int32, (256, 128), 0) // 64
    head_of_lane = lax.broadcasted_iota(jnp.int32, (256, 128), 1) // 32
    block_mask = head_of_row == head_of_lane
    lane = lax.broadcasted_iota(jnp.int32, (128, 128), 1)
    zero = jnp.zeros((64, 128), BF16)

    def spread_heads(tile):
        return jnp.where(block_mask, jnp.concatenate([tile] * 4, axis=0), jnp.zeros((256, 128), BF16))

    for pair in range(4):
        row_a, row_b = (128 * pair, 128 * pair + 64)
        total = None
        for j in range(3):
            def part_of(part, row):
                return qkv[row : row + 64, part * GF + 128 * j : part * GF + 128 * (j + 1)]

            query = jnp.concatenate(
                [
                    jnp.concatenate([part_of(0, row_a), zero], axis=1),
                    jnp.concatenate([zero, part_of(0, row_b)], axis=1),
                ],
                axis=0,
            )
            key = jnp.concatenate(
                [spread_heads(part_of(1, row_a)), spread_heads(part_of(1, row_b))], axis=1
            )
            scores = dot(key, query, NT) * HS ** (-0.5) + bias_ref[256 * j : 256 * (j + 1)]
            scores = scores.reshape(4, 64, 128)
            powers = jnp.exp(scores - jnp.max(scores, axis=1, keepdims=True))
            chances = powers * (1.0 / jnp.sum(powers, axis=1, keepdims=True))
            chances = chances.reshape(256, 128).astype(BF16)
            value = jnp.concatenate(
                [
                    dot(folded_t[j], spread_heads(part_of(2, row_a)), NT),
                    dot(folded_t[j], spread_heads(part_of(2, row_b)), NT),
                ],
                axis=0,
            ).astype(BF16)
            term = dot(value, chances)
            total = term if total is None else total + term
        decoded = jnp.where(lane < 64, total[:128], total[128:]).T
        if pair < 2:
            decoded = decoded + residual_ref[128 * pair : 128 * (pair + 1)]
        fields[128 * pair : 128 * (pair + 1)] = decoded
    cell = lax.broadcasted_iota(jnp.int32, (8, 128), 0)
    for tile in range(16):
        for block in range(2):
            for side in range(2):
                at = 2 + 2 * side + block
                code = jnp.broadcast_to(observed_ref[tile, at : at + 1].astype(jnp.int32), (8, 128))
                channel, place = (code & 127, code >> 7)
                for member in range(2):
                    found = None
                    for half in range(2):
                        row = member * 256 + 16 * tile + 8 * half
                        gathered = jnp.take_along_axis(fields[row : row + 8], channel, axis=1)
                        kept = jnp.where(place == cell + 8 * half, gathered, 0.0)
                        found = kept if found is None else found + kept
                    found = -jnp.sum(found, axis=0, keepdims=True)
                    if side == 0 and member == 0:
                        found = found + observed_ref[tile, block : block + 1]
                    row = 32 * side + 2 * tile + block
                    sums[row : row + 1, 128 * member : 128 * (member + 1)] = found
    both = sums[...].astype(BF16)
    both_ref[...] = both
    right_ref[...] = both[:32]
    left_ref[...] = both[32:]


def decode_kernel(observed_ref, out_ref):
    index = observed_ref[...]
    line = jnp.where(index >= WIN * CH, 1.0, 0.0)
    rest = index - line * (WIN * CH)
    column = jnp.floor((rest + 0.5) * (1.0 / CH))
    channel = rest - column * CH
    side = lax.broadcasted_iota(jnp.int32, index.shape, 1)
    late = column >= SHIFT
    place = line * WIN + jnp.where(late, column - SHIFT, column + SHIFT)
    inside = late == (side < 4)
    place = jnp.where(inside, place, 64.0)
    out_ref[...] = jnp.where(side < 2, index, place * 128.0 + channel)


def select_kernel(chosen_ref, own_ref, prev_ref, next_ref, second_ref, out_ref, table, picked):
    for place, part in enumerate(
        (prev_ref[:32], own_ref[:32], next_ref[...], second_ref[...], prev_ref[32:], own_ref[32:])
    ):
        table[32 * place : 32 * (place + 1)] = part.astype(F32)
    table[192:200] = jnp.zeros((8, 256), F32)
    table[288:296] = jnp.zeros((8, 256), F32)
    for band in range(16):
        for j in range(MAXL):
            row = chosen_ref[MAXL * band + j]
            found = table[pl.ds(row, 1)] + table[pl.ds(row + 96, 1)]
            for member in range(2):
                to = MAXL * member + j
                picked[band, to : to + 1] = found[:, 128 * member : 128 * (member + 1)]
    out_ref[...] = picked[...].astype(BF16)


def update_kernel(arrived_ref, gains_ref, out_ref):
    row = lax.broadcasted_iota(jnp.int32, (64, 128), 0)
    col = lax.broadcasted_iota(jnp.int32, (64, 128), 1)
    entry, member = (row // 16, row % 16)
    source, pair, source_entry = (col // 8, (col // 4) % 2, col % 4)
    same = (entry == source_entry) & ((source ^ pair) == member)
    gather = jnp.where(same, 1.0, 0.0).astype(BF16)
    chosen = dot(gather, arrived_ref[...].reshape(128, 128)).astype(BF16)
    total = None
    for j in range(4):
        term = dot(chosen[16 * j : 16 * (j + 1)], gains_ref[j], NT)
        total = term if total is None else total + term
    out_ref[...] = total


def shift(x, by):
    peers = lax.axis_size(SPACE)
    return lax.ppermute(x, SPACE, [(i, (i + by) % peers) for i in range(peers)])


def swap_pairs(first):
    pairs = []
    for y in range(8):
        for core in range(2):
            odd_pairing = (core == 0) != first
            other = (y ^ 1) if not odd_pairing else ((y + 1) % 8 if y % 2 else (y - 1) % 8)
            pairs.append((2 * y + core, 2 * other + core))
    return pairs


def swap_index(y, core, first):
    odd_pairing = (core == 0) != first
    even = jnp.where(y % 2 == 1, y - 1, y + 1)
    odd = jnp.where(y % 2 == 1, (y + 1) % 8, (y + 7) % 8)
    return jnp.where(odd_pairing, odd, even)


def core_swap(x):
    return lax.ppermute(x, "core", [(0, 1), (1, 0)])


def block_starts(y, core):
    starts = []
    for of_core in (core, 1 - core):
        places = [y, swap_index(y, of_core, True)]
        for chain in ([False], [True, False], [False, True, False]):
            at = y
            for step in chain:
                at = swap_index(at, of_core, step)
            places += [at, swap_index(at, of_core, True)]
        starts += [place * 96 + of_core * 48 for place in places]
    return jnp.stack(starts).astype(jnp.int32)


def smem():
    return pl.BlockSpec(memory_space=pltpu.SMEM)


def vmem():
    return pl.BlockSpec(memory_space=pltpu.VMEM)


def params(limit=VMEM_LIMIT):
    return pltpu.CompilerParams(vmem_limit_bytes=limit)


def body(
    tokens,
    norm_gain,
    w_qkv,
    w_out,
    rel_bias,
    w_decode,
    obs_value,
    obs_pert,
    obs_index,
    block_list,
    list_count,
    gains,
):
    features = tokens.shape[3]
    group = (lax.axis_index("x") % 2).astype(jnp.int32)
    w_decode_t = w_decode.T

    rows = pl.pallas_call(
        weights_kernel,
        out_shape=jax.ShapeDtypeStruct((w_qkv.shape[0], WCOLS), BF16),
        in_specs=[smem(), vmem(), vmem(), vmem()],
        out_specs=vmem(),
        compiler_params=params(63 * 1024 * 1024),
        name="weights",
    )(group.reshape(1), w_qkv, w_out, w_decode_t)
    core, low, y = (lax.axis_index("core"), lax.axis_index("zlo"), lax.axis_index("y"))
    far = lax.ppermute(rows, "zlo", [(0, 1), (1, 0)])
    block = jnp.where(
        low == 0, jnp.concatenate([rows, far], axis=0), jnp.concatenate([far, rows], axis=0)
    )
    first, second = (swap_pairs(True), swap_pairs(False))
    near = lax.ppermute(block, ROW, first)

    edge = pl.pallas_call(
        edge_kernel,
        out_shape=jax.ShapeDtypeStruct((32 * SHIFT + 16, features), BF16),
        in_specs=[vmem(), vmem()],
        out_specs=vmem(),
        compiler_params=params(),
        name="edge",
    )(tokens, obs_index[0, 0])
    halo = shift(edge, -1)
    near, halo = lax.optimization_barrier((near, halo))
    held = [jnp.concatenate([block, near], axis=0)]
    held.append(lax.ppermute(held[0], ROW, second))
    normed, notes = pl.pallas_call(
        norm_kernel,
        grid=(4,),
        out_shape=(
            jax.ShapeDtypeStruct((256, features), BF16),
            jax.ShapeDtypeStruct((16, 8, 128), F32),
        ),
        in_specs=[
            smem(),
            smem(),
            pl.BlockSpec((1, WIN, WIN, features), lambda i: (0, i, 0, 0)),
            pl.BlockSpec((WIN * SHIFT, features), lambda i: (i, 0)),
            pl.BlockSpec((16, features), lambda i: (8, 0)),
            pl.BlockSpec((1, features), lambda i: (0, 0)),
            pl.BlockSpec((2, 128), lambda i: (0, 0)),
            pl.BlockSpec((16, 2, 128), lambda i: (0, 0, 0)),
            pl.BlockSpec((2, 128), lambda i: (0, 0)),
        ],
        out_specs=(
            pl.BlockSpec((64, features), lambda i: (i, 0)),
            pl.BlockSpec((16, 8, 128), lambda i: (0, 0, 0)),
        ),
        compiler_params=params(),
        name="norm",
    )(
        block_list[0, 0],
        list_count[0],
        tokens,
        halo,
        halo,
        norm_gain.reshape(1, -1),
        obs_value[0, 0],
        obs_pert[:, 0, 0],
        obs_index[0, 0],
    )
    mate = lax.ppermute(normed, "x", [(0, 1), (1, 0), (2, 3), (3, 2)])
    bias = pl.pallas_call(
        bias_kernel,
        grid_spec=pltpu.PrefetchScalarGridSpec(
            num_scalar_prefetch=1,
            grid=(1,),
            in_specs=[pl.BlockSpec((GROUP_HEADS, 64, 64), lambda i, group: (group[0], 0, 0))],
            out_specs=pl.BlockSpec((GROUP_HEADS * 64, 128), lambda i, group: (0, 0)),
        ),
        out_shape=jax.ShapeDtypeStruct((GROUP_HEADS * 64, 128), F32),
        compiler_params=params(),
        name="bias",
    )(group.reshape(1), rel_bias)
    starts = block_starts(y, core)
    held[1], bias, starts, _ = lax.optimization_barrier((held[1], bias, starts, normed))
    held.append(lax.ppermute(held[1], ROW, first))
    halo, _ = lax.optimization_barrier((halo, held[1]))
    own, residual = pl.pallas_call(
        own_kernel,
        grid=(4,),
        out_shape=(
            jax.ShapeDtypeStruct((256, features), BF16),
            jax.ShapeDtypeStruct((256, 128), F32),
        ),
        in_specs=[
            pl.BlockSpec((1, WIN, WIN, features), lambda i: (0, i, 0, 0)),
            pl.BlockSpec((WIN * SHIFT, features), lambda i: (i, 0)),
            pl.BlockSpec((1, features), lambda i: (0, 0)),
            pl.BlockSpec(w_decode_t.shape, lambda i: (0, 0)),
        ],
        out_specs=(
            pl.BlockSpec((64, features), lambda i: (i, 0)),
            pl.BlockSpec((64, 128), lambda i: (i, 0)),
        ),
        compiler_params=params(),
        name="own",
    )(tokens, halo, norm_gain.reshape(1, -1), w_decode_t)
    swapped = [core_swap(held[0]), core_swap(held[1])]
    held[2], swapped[0], own, residual = lax.optimization_barrier((held[2], swapped[0], own, residual))
    held.append(lax.ppermute(held[2], ROW, second))
    swapped.append(core_swap(held[2]))

    notes, _ = lax.optimization_barrier((notes, held[2]))
    observed = lax.all_to_all(notes, MEMBER, split_axis=0, concat_axis=0, tiled=True)
    entries = pl.pallas_call(
        decode_kernel,
        out_shape=jax.ShapeDtypeStruct((16, 8, 128), F32),
        in_specs=[vmem()],
        out_specs=vmem(),
        cost_estimate=pl.CostEstimate(flops=4 * 10**9, bytes_accessed=10**6, transcendentals=0),
        compiler_params=params(),
        name="decode",
    )(observed)
    last, mate, swapped[1] = lax.optimization_barrier((held[3], mate, swapped[1]))
    swapped.append(core_swap(last))
    blocks = held + swapped

    meta = observed[:, 6].astype(jnp.int32)
    listed, count = (meta[:, :MAXL], meta[:, MAXL : MAXL + 1])
    band = jnp.arange(16)[:, None] + listed // 6 - 1
    live = (jnp.arange(MAXL)[None] < count) & (band >= 0) & (band < 16)
    chosen = jnp.where(live, (listed // 2 % 3) * 32 + band * 2 + listed % 2, 192).reshape(16 * MAXL)

    both, right, left = pl.pallas_call(
        attention_kernel,
        out_shape=(
            jax.ShapeDtypeStruct((64, 256), BF16),
            jax.ShapeDtypeStruct((32, 256), BF16),
            jax.ShapeDtypeStruct((32, 256), BF16),
        ),
        in_specs=[
            smem(),
            smem(),
            vmem(),
            vmem(),
            vmem(),
            [vmem()] * 8,
            vmem(),
            vmem(),
        ],
        out_specs=(vmem(), vmem(), vmem()),
        scratch_shapes=[
            pltpu.VMEM((features, WCOLS), BF16),
            pltpu.VMEM((512, 3 * GF), BF16),
            pltpu.VMEM((512, 128), F32),
            pltpu.VMEM((64, 256), F32),
        ],
        compiler_params=params(48 * 1024 * 1024),
        name="attention",
    )(group.reshape(1), starts, own, mate, residual, blocks, bias, entries)

    previous, following, second = (shift(both, 1), shift(right, -1), shift(left, 2))
    selected = pl.pallas_call(
        select_kernel,
        out_shape=jax.ShapeDtypeStruct((16, 8, 128), BF16),
        in_specs=[smem()] + [vmem()] * 4,
        out_specs=vmem(),
        scratch_shapes=[pltpu.VMEM((296, 256), F32), pltpu.VMEM((16, 8, 128), F32)],
        compiler_params=params(),
        name="select",
    )(chosen, both, previous, following, second)
    arrived = lax.all_to_all(selected, MEMBER, split_axis=0, concat_axis=0, tiled=True)
    gains_t = gains[0, 0].transpose(0, 2, 1)
    increment = pl.pallas_call(
        update_kernel,
        out_shape=jax.ShapeDtypeStruct((16, gains.shape[4]), F32),
        in_specs=[vmem(), vmem()],
        out_specs=vmem(),
        compiler_params=params(),
        name="update",
    )(arrived, gains_t)
    return increment[None, None]


def solution(mesh):
    fine = Mesh(np.asarray(mesh.devices).reshape(4, 4, 2, 8, 2), ("zhi", "x", "zlo", "y", "core"))
    in_specs = (
        P(MEMBER, None, SPACE, None),
        P(),
        P(SPACE, None),
        P(SPACE, None),
        P(),
        P(),
        P(MEMBER, SPACE, None, None),
        P(None, MEMBER, SPACE, None, None),
        P(MEMBER, SPACE, None, None),
        P(MEMBER, SPACE, None),
        P(MEMBER, SPACE),
        P(MEMBER, SPACE, None, None, None),
    )
    out_specs = P(MEMBER, SPACE, None, None)
    return jax.shard_map(body, mesh=fine, in_specs=in_specs, out_specs=out_specs, check_vma=False)
```

```python
import jax
import jax.numpy as jnp
import numpy as np
from jax import lax
from jax.experimental import pallas as pl
from jax.experimental.pallas import tpu as pltpu
from jax.sharding import Mesh, PartitionSpec as P

HEADS = 24
HS = 32
WIN = 8
SHIFT = 4
MAXL = 4
CH = 69
MEMBER = ("zhi", "x")
SPACE = ("zlo", "y", "core")
ROW = ("y", "core")
GROUP_HEADS = 12
GF = GROUP_HEADS * HS
WCOLS = 3 * GF + 128
F32 = jnp.float32
BF16 = jnp.bfloat16
NT = (((1,), (1,)), ((), ()))
VMEM_LIMIT = 8 * 1024 * 1024


def dot(a, b, dims=(((1,), (0,)), ((), ()))):
    return lax.dot_general(a, b, dims, preferred_element_type=F32)


def weights_kernel(group_ref, w_qkv_ref, w_out_ref, w_decode_ref, out_ref):
    for group in range(2):

        @pl.when(group_ref[0] == group)
        def _():
            for part in range(3):
                out_ref[:, part * GF : (part + 1) * GF] = w_qkv_ref[
                    :, (2 * part + group) * GF : (2 * part + group + 1) * GF
                ]

    folded = dot(w_out_ref[...], w_decode_ref[...], NT)
    rows, channels = folded.shape
    wide = jnp.concatenate([folded, jnp.zeros((rows, 128 - channels), F32)], axis=1)
    full = jnp.concatenate([wide, jnp.zeros((out_ref.shape[0] - rows, 128), F32)], axis=0)
    out_ref[:, 3 * GF :] = full.astype(BF16)


def edge_kernel(tokens_ref, index_ref, out_ref):
    tile = tokens_ref[0].astype(F32)
    lines, _, features = tile.shape
    tile = tile.reshape(lines // 2, 2, WIN, features)
    spot = lax.broadcasted_iota(jnp.int32, (lines // 2, WIN, features), 1)
    packed = jnp.where(spot < SHIFT, tile[:, 0], pltpu.roll(tile[:, 1], 4, axis=1))
    rows = lines * SHIFT
    out_ref[:rows] = packed.reshape(rows, features).astype(BF16)
    index = index_ref[...]
    upper = (index // 32).astype(F32)
    lower = (index % 32).astype(F32)
    wide = jnp.concatenate(
        [upper[:1], upper[1:], lower[:1], lower[1:], jnp.zeros((1, features - 512), F32)], axis=1
    )
    out_ref[rows:] = jnp.broadcast_to(wide, (16, features)).astype(BF16)


def bias_kernel(group_ref, rel_bias_ref, out_ref):
    for head in range(GROUP_HEADS):
        turned = rel_bias_ref[head].T
        out_ref[64 * head : 64 * (head + 1)] = jnp.concatenate([turned, turned], axis=1)


def norm_kernel(
    list_ref,
    count_ref,
    tokens_ref,
    halo_ref,
    extra_ref,
    gain_ref,
    w_decode_ref,
    value_ref,
    pert_ref,
    index_ref,
    normed_ref,
    residual_ref,
    notes_ref,
):
    @pl.when(pl.program_id(0) == 0)
    def _():
        parts = extra_ref[:8].astype(F32)
        following = [parts[:1, 128 * b : 128 * (b + 1)] * 32.0 + parts[:1, 256 + 128 * b : 384 + 128 * b] for b in range(2)]
        lane = lax.broadcasted_iota(jnp.int32, (1, 128), 1)
        listed = jnp.where(lane == MAXL, count_ref[0], 0)
        for j in range(MAXL):
            listed = jnp.where(lane == j, list_ref[j], listed)
        same = jnp.concatenate(
            [index_ref[...].astype(F32)] + following + [listed.astype(F32), jnp.zeros((1, 128), F32)], axis=0
        )
        for member in range(16):
            notes_ref[member] = jnp.concatenate([value_ref[...] + pert_ref[member], same], axis=0)

    own = tokens_ref[0].astype(F32)
    halo = halo_ref[...].astype(F32)
    features = own.shape[-1]
    halo = halo.reshape(WIN // 2, WIN, features)
    halo = jnp.stack([pltpu.roll(halo, 4, axis=1), halo], axis=1).reshape(WIN, WIN, features)
    spot = lax.broadcasted_iota(jnp.int32, (WIN, WIN, features), 1)
    window = jnp.where(spot < SHIFT, pltpu.roll(own, 4, axis=1), halo).reshape(WIN * WIN, features)
    center = jnp.mean(window, axis=-1, keepdims=True)
    spread = jnp.mean((window - center) ** 2, axis=-1, keepdims=True)
    normed = (window - center) * lax.rsqrt(spread + 1e-05) * gain_ref[...]
    normed_ref[...] = normed.astype(BF16)
    residual = dot(window.astype(BF16), w_decode_ref[...], NT)
    residual_ref[...] = jnp.concatenate(
        [residual, jnp.zeros((WIN * WIN, 128 - CH), F32)], axis=1
    )


def attention_kernel(
    group_ref,
    starts_ref,
    own_ref,
    mate_ref,
    residual_ref,
    blocks,
    bias_ref,
    observed_ref,
    both_ref,
    right_ref,
    left_ref,
    weights,
    qkv,
    fields,
    sums,
):
    for i, block in enumerate(blocks):
        for half in range(2):
            for low in range(2):
                start = pl.multiple_of(starts_ref[2 * i + half] + 768 * low, 48)
                row = 96 * half + 48 * low
                weights[pl.ds(start, 48), :] = block[row : row + 48]
    for part in range(3):
        lanes = slice(part * GF, (part + 1) * GF)
        for member, source in enumerate((own_ref, mate_ref)):
            qkv[member * 256 : (member + 1) * 256, lanes] = dot(source[...], weights[:, lanes]).astype(BF16)
    first = pl.multiple_of(group_ref[0] * 768, 768)
    folded = jnp.concatenate(
        [
            weights[pl.ds(pl.multiple_of(first + 48 * t, 48), 48), 3 * GF :].astype(F32)[:24]
            for t in range(16)
        ],
        axis=0,
    )
    folded_t = [folded[128 * j : 128 * (j + 1)].T.astype(BF16) for j in range(3)]
    head_of_row = lax.broadcasted_iota(jnp.int32, (256, 128), 0) // 64
    head_of_lane = lax.broadcasted_iota(jnp.int32, (256, 128), 1) // 32
    block_mask = head_of_row == head_of_lane
    lane = lax.broadcasted_iota(jnp.int32, (128, 128), 1)
    zero = jnp.zeros((64, 128), BF16)

    def spread_heads(tile):
        return jnp.where(block_mask, jnp.concatenate([tile] * 4, axis=0), jnp.zeros((256, 128), BF16))

    for pair in range(4):
        row_a, row_b = (128 * pair, 128 * pair + 64)
        total = None
        for j in range(3):
            def part_of(part, row):
                return qkv[row : row + 64, part * GF + 128 * j : part * GF + 128 * (j + 1)]

            query = jnp.concatenate(
                [
                    jnp.concatenate([part_of(0, row_a), zero], axis=1),
                    jnp.concatenate([zero, part_of(0, row_b)], axis=1),
                ],
                axis=0,
            )
            key = jnp.concatenate(
                [spread_heads(part_of(1, row_a)), spread_heads(part_of(1, row_b))], axis=1
            )
            scores = dot(key, query, NT) * HS ** (-0.5) + bias_ref[256 * j : 256 * (j + 1)]
            scores = scores.reshape(4, 64, 128)
            powers = jnp.exp(scores - jnp.max(scores, axis=1, keepdims=True))
            chances = powers * (1.0 / jnp.sum(powers, axis=1, keepdims=True))
            chances = chances.reshape(256, 128).astype(BF16)
            value = jnp.concatenate(
                [
                    dot(folded_t[j], spread_heads(part_of(2, row_a)), NT),
                    dot(folded_t[j], spread_heads(part_of(2, row_b)), NT),
                ],
                axis=0,
            ).astype(BF16)
            term = dot(value, chances)
            total = term if total is None else total + term
        decoded = jnp.where(lane < 64, total[:128], total[128:]).T
        if pair < 2:
            decoded = decoded + residual_ref[128 * pair : 128 * (pair + 1)]
        fields[128 * pair : 128 * (pair + 1)] = decoded
    cell = lax.broadcasted_iota(jnp.int32, (8, 128), 0)
    for tile in range(16):
        for block in range(2):
            for side in range(2):
                at = 2 + 2 * side + block
                code = jnp.broadcast_to(observed_ref[tile, at : at + 1].astype(jnp.int32), (8, 128))
                channel, place = (code & 127, code >> 7)
                for member in range(2):
                    found = None
                    for half in range(2):
                        row = member * 256 + 16 * tile + 8 * half
                        gathered = jnp.take_along_axis(fields[row : row + 8], channel, axis=1)
                        kept = jnp.where(place == cell + 8 * half, gathered, 0.0)
                        found = kept if found is None else found + kept
                    found = -jnp.sum(found, axis=0, keepdims=True)
                    if side == 0 and member == 0:
                        found = found + observed_ref[tile, block : block + 1]
                    row = 32 * side + 2 * tile + block
                    sums[row : row + 1, 128 * member : 128 * (member + 1)] = found
    both = sums[...].astype(BF16)
    both_ref[...] = both
    right_ref[...] = both[:32]
    left_ref[...] = both[32:]


def decode_kernel(observed_ref, out_ref):
    index = observed_ref[...]
    line = jnp.where(index >= WIN * CH, 1.0, 0.0)
    rest = index - line * (WIN * CH)
    column = jnp.floor((rest + 0.5) * (1.0 / CH))
    channel = rest - column * CH
    side = lax.broadcasted_iota(jnp.int32, index.shape, 1)
    late = column >= SHIFT
    place = line * WIN + jnp.where(late, column - SHIFT, column + SHIFT)
    inside = late == (side < 4)
    place = jnp.where(inside, place, 64.0)
    out_ref[...] = jnp.where(side < 2, index, place * 128.0 + channel)


def select_kernel(chosen_ref, own_ref, prev_ref, next_ref, second_ref, out_ref, table, picked):
    parts = (
        (prev_ref[:32], second_ref[...]),
        (own_ref[:32], prev_ref[32:]),
        (next_ref[...], own_ref[32:]),
    )
    for place, (late, early) in enumerate(parts):
        table[32 * place : 32 * (place + 1)] = late.astype(F32) + early.astype(F32)
    table[96:104] = jnp.zeros((8, 256), F32)
    for band in range(16):
        for j in range(MAXL):
            found = table[pl.ds(chosen_ref[MAXL * band + j], 1)]
            for member in range(2):
                to = MAXL * member + j
                picked[band, to : to + 1] = found[:, 128 * member : 128 * (member + 1)]
    out_ref[...] = picked[...].astype(BF16)


def update_kernel(arrived_ref, gains_ref, out_ref):
    row = lax.broadcasted_iota(jnp.int32, (64, 128), 0)
    col = lax.broadcasted_iota(jnp.int32, (64, 128), 1)
    entry, member = (row // 16, row % 16)
    source, pair, source_entry = (col // 8, (col // 4) % 2, col % 4)
    same = (entry == source_entry) & ((source ^ pair) == member)
    gather = jnp.where(same, 1.0, 0.0).astype(BF16)
    chosen = dot(gather, arrived_ref[...].reshape(128, 128)).astype(BF16)
    total = None
    for j in range(4):
        term = dot(chosen[16 * j : 16 * (j + 1)], gains_ref[j], NT)
        total = term if total is None else total + term
    out_ref[...] = total


def shift(x, by):
    peers = lax.axis_size(SPACE)
    return lax.ppermute(x, SPACE, [(i, (i + by) % peers) for i in range(peers)])


def swap_pairs(first):
    pairs = []
    for y in range(8):
        for core in range(2):
            odd_pairing = (core == 0) != first
            other = (y ^ 1) if not odd_pairing else ((y + 1) % 8 if y % 2 else (y - 1) % 8)
            pairs.append((2 * y + core, 2 * other + core))
    return pairs


def swap_index(y, core, first):
    odd_pairing = (core == 0) != first
    even = jnp.where(y % 2 == 1, y - 1, y + 1)
    odd = jnp.where(y % 2 == 1, (y + 1) % 8, (y + 7) % 8)
    return jnp.where(odd_pairing, odd, even)


def core_swap(x):
    return lax.ppermute(x, "core", [(0, 1), (1, 0)])


def block_starts(y, core):
    starts = []
    for of_core in (core, 1 - core):
        places = [y, swap_index(y, of_core, True)]
        for chain in ([False], [True, False], [False, True, False]):
            at = y
            for step in chain:
                at = swap_index(at, of_core, step)
            places += [at, swap_index(at, of_core, True)]
        starts += [place * 96 + of_core * 48 for place in places]
    return jnp.stack(starts).astype(jnp.int32)


def smem():
    return pl.BlockSpec(memory_space=pltpu.SMEM)


def vmem():
    return pl.BlockSpec(memory_space=pltpu.VMEM)


def params(limit=VMEM_LIMIT):
    return pltpu.CompilerParams(vmem_limit_bytes=limit)


def body(
    tokens,
    norm_gain,
    w_qkv,
    w_out,
    rel_bias,
    w_decode,
    obs_value,
    obs_pert,
    obs_index,
    block_list,
    list_count,
    gains,
):
    features = tokens.shape[3]
    group = (lax.axis_index("x") % 2).astype(jnp.int32)
    w_decode_t = w_decode.T

    rows = pl.pallas_call(
        weights_kernel,
        out_shape=jax.ShapeDtypeStruct((w_qkv.shape[0], WCOLS), BF16),
        in_specs=[smem(), vmem(), vmem(), vmem()],
        out_specs=vmem(),
        compiler_params=params(63 * 1024 * 1024),
        name="weights",
    )(group.reshape(1), w_qkv, w_out, w_decode_t)
    core, low, y = (lax.axis_index("core"), lax.axis_index("zlo"), lax.axis_index("y"))
    far = lax.ppermute(rows, "zlo", [(0, 1), (1, 0)])
    block = jnp.where(
        low == 0, jnp.concatenate([rows, far], axis=0), jnp.concatenate([far, rows], axis=0)
    )
    first, second = (swap_pairs(True), swap_pairs(False))
    near = lax.ppermute(block, ROW, first)

    edge = pl.pallas_call(
        edge_kernel,
        out_shape=jax.ShapeDtypeStruct((32 * SHIFT + 16, features), BF16),
        in_specs=[vmem(), vmem()],
        out_specs=vmem(),
        compiler_params=params(),
        name="edge",
    )(tokens, obs_index[0, 0])
    halo = shift(edge, -1)
    near, halo = lax.optimization_barrier((near, halo))
    held = [jnp.concatenate([block, near], axis=0)]
    held.append(lax.ppermute(held[0], ROW, second))
    normed, residual, notes = pl.pallas_call(
        norm_kernel,
        grid=(4,),
        out_shape=(
            jax.ShapeDtypeStruct((256, features), BF16),
            jax.ShapeDtypeStruct((256, 128), F32),
            jax.ShapeDtypeStruct((16, 8, 128), F32),
        ),
        in_specs=[
            smem(),
            smem(),
            pl.BlockSpec((1, WIN, WIN, features), lambda i: (0, i, 0, 0)),
            pl.BlockSpec((WIN * SHIFT, features), lambda i: (i, 0)),
            pl.BlockSpec((16, features), lambda i: (8, 0)),
            pl.BlockSpec((1, features), lambda i: (0, 0)),
            pl.BlockSpec(w_decode_t.shape, lambda i: (0, 0)),
            pl.BlockSpec((2, 128), lambda i: (0, 0)),
            pl.BlockSpec((16, 2, 128), lambda i: (0, 0, 0)),
            pl.BlockSpec((2, 128), lambda i: (0, 0)),
        ],
        out_specs=(
            pl.BlockSpec((64, features), lambda i: (i, 0)),
            pl.BlockSpec((64, 128), lambda i: (i, 0)),
            pl.BlockSpec((16, 8, 128), lambda i: (0, 0, 0)),
        ),
        compiler_params=params(),
        name="norm",
    )(
        block_list[0, 0],
        list_count[0],
        tokens,
        halo,
        halo,
        norm_gain.reshape(1, -1),
        w_decode_t,
        obs_value[0, 0],
        obs_pert[:, 0, 0],
        obs_index[0, 0],
    )
    mate = lax.ppermute(normed, "x", [(0, 1), (1, 0), (2, 3), (3, 2)])
    bias = pl.pallas_call(
        bias_kernel,
        grid_spec=pltpu.PrefetchScalarGridSpec(
            num_scalar_prefetch=1,
            grid=(1,),
            in_specs=[pl.BlockSpec((GROUP_HEADS, 64, 64), lambda i, group: (group[0], 0, 0))],
            out_specs=pl.BlockSpec((GROUP_HEADS * 64, 128), lambda i, group: (0, 0)),
        ),
        out_shape=jax.ShapeDtypeStruct((GROUP_HEADS * 64, 128), F32),
        compiler_params=params(),
        name="bias",
    )(group.reshape(1), rel_bias)
    starts = block_starts(y, core)
    held[1], bias, starts, _ = lax.optimization_barrier((held[1], bias, starts, normed))
    held.append(lax.ppermute(held[1], ROW, first))
    swapped = [core_swap(held[0]), core_swap(held[1])]
    held[2], swapped[0] = lax.optimization_barrier((held[2], swapped[0]))
    held.append(lax.ppermute(held[2], ROW, second))
    swapped.append(core_swap(held[2]))

    notes, _ = lax.optimization_barrier((notes, held[2]))
    observed = lax.all_to_all(notes, MEMBER, split_axis=0, concat_axis=0, tiled=True)
    entries = pl.pallas_call(
        decode_kernel,
        out_shape=jax.ShapeDtypeStruct((16, 8, 128), F32),
        in_specs=[vmem()],
        out_specs=vmem(),
        cost_estimate=pl.CostEstimate(flops=4 * 10**9, bytes_accessed=10**6, transcendentals=0),
        compiler_params=params(),
        name="decode",
    )(observed)
    last, mate, swapped[1] = lax.optimization_barrier((held[3], mate, swapped[1]))
    swapped.append(core_swap(last))
    blocks = held + swapped

    meta = observed[:, 6].astype(jnp.int32)
    listed, count = (meta[:, :MAXL], meta[:, MAXL : MAXL + 1])
    band = jnp.arange(16)[:, None] + listed // 6 - 1
    live = (jnp.arange(MAXL)[None] < count) & (band >= 0) & (band < 16)
    chosen = jnp.where(live, (listed // 2 % 3) * 32 + band * 2 + listed % 2, 96).reshape(16 * MAXL)

    both, right, left = pl.pallas_call(
        attention_kernel,
        out_shape=(
            jax.ShapeDtypeStruct((64, 256), BF16),
            jax.ShapeDtypeStruct((32, 256), BF16),
            jax.ShapeDtypeStruct((32, 256), BF16),
        ),
        in_specs=[
            smem(),
            smem(),
            vmem(),
            vmem(),
            vmem(),
            [vmem()] * 8,
            vmem(),
            vmem(),
        ],
        out_specs=(vmem(), vmem(), vmem()),
        scratch_shapes=[
            pltpu.VMEM((features, WCOLS), BF16),
            pltpu.VMEM((512, 3 * GF), BF16),
            pltpu.VMEM((512, 128), F32),
            pltpu.VMEM((64, 256), F32),
        ],
        compiler_params=params(48 * 1024 * 1024),
        name="attention",
    )(group.reshape(1), starts, normed, mate, residual, blocks, bias, entries)

    previous, following, second = (shift(both, 1), shift(right, -1), shift(left, 2))
    selected = pl.pallas_call(
        select_kernel,
        out_shape=jax.ShapeDtypeStruct((16, 8, 128), BF16),
        in_specs=[smem()] + [vmem()] * 4,
        out_specs=vmem(),
        scratch_shapes=[pltpu.VMEM((104, 256), F32), pltpu.VMEM((16, 8, 128), F32)],
        compiler_params=params(),
        name="select",
    )(chosen, both, previous, following, second)
    arrived = lax.all_to_all(selected, MEMBER, split_axis=0, concat_axis=0, tiled=True)
    gains_t = gains[0, 0].transpose(0, 2, 1)
    increment = pl.pallas_call(
        update_kernel,
        out_shape=jax.ShapeDtypeStruct((16, gains.shape[4]), F32),
        in_specs=[vmem(), vmem()],
        out_specs=vmem(),
        compiler_params=params(),
        name="update",
    )(arrived, gains_t)
    return increment[None, None]


def solution(mesh):
    fine = Mesh(np.asarray(mesh.devices).reshape(4, 4, 2, 8, 2), ("zhi", "x", "zlo", "y", "core"))
    in_specs = (
        P(MEMBER, None, SPACE, None),
        P(),
        P(SPACE, None),
        P(SPACE, None),
        P(),
        P(),
        P(MEMBER, SPACE, None, None),
        P(None, MEMBER, SPACE, None, None),
        P(MEMBER, SPACE, None, None),
        P(MEMBER, SPACE, None),
        P(MEMBER, SPACE),
        P(MEMBER, SPACE, None, None, None),
    )
    out_specs = P(MEMBER, SPACE, None, None)
    return jax.shard_map(body, mesh=fine, in_specs=in_specs, out_specs=out_specs, check_vma=False)
```
